32 devices in a mesh: groups: 2 (over x), pos: 8 (over z, y), mp: 2 (over core).
Axes of the slice: x: 2, y: 2, z: 4, core: 2. Of those that a mesh axis runs over, the one named last changes fastest.
Arguments:
- gate_stream: bfloat16 [8192, 4096], P(('groups', 'pos'), 'mp'), parts along dimension 0, may hold values from -6 to 6
- key_stream: bfloat16 [8192, 4096], P(('groups', 'pos'), 'mp'), parts along dimension 0, may hold values from -6 to 6
- value_stream: bfloat16 [8192, 4096], P(('groups', 'pos'), 'mp'), parts along dimension 0, may hold values from -6 to 6
- filters: float32 [4096, 128], P('mp')
- temps: float32 [32], P('mp'), may hold values from 4 to 24
- queries: bfloat16 [32, 256, 4096], P('groups', 'pos', 'mp'), parts along dimension 0, may hold values from -6 to 6
- blocks: int32 [32], P('groups'), parts along dimension 0, may hold values from 0 to 7, as said below
- sites: int32 [32], P('groups'), parts along dimension 0, may hold values from 128 to 4095, as said below
Outputs:
- hyena_out: bfloat16 [8192, 4096], P(('groups', 'pos'), 'mp'), parts along dimension 0
- attended: bfloat16 [32, 256, 4096], P('groups', 'pos', 'mp'), parts along dimension 0
The draws below stay inside these ranges and needn't reach their ends.
There are 2 independent parts, one for each index of `groups`. The reference program is written for one: setup_inputs(seed, part) draws one part's arguments, and reference() takes and returns one part's arrays. A program takes and returns all parts, laid end to end along the dimension named above; an argument that names none is the same for every part. Nothing has to cross between parts.
Inputs may be any that keep to these rules, and one draw needn't show every extreme that they name: `blocks`: A block is the 512 reference positions of one index of pos. Exactly one block is named by exactly 4 windows; every other block by at most two windows, and some block by exactly two. sites[w] - 512 * blocks[w] lies from 128 to 511.
All inputs are finite; a program needn't handle non-finite values.
Results may differ from the reference program's by a relative error of at most 0.01.
Values may be sent and summed in bfloat16 or wider, within the bound.
No kernel may reach another device: no remote copies, remote signals or barrier semaphores. Data moves between devices by JAX's collectives and lax.ppermute only.
A program may use at most 128 MiB of HBM per device.

```python
import math
import jax
import jax.numpy as jnp
from jax import lax

HEADS = 32
HEAD_DIM = 128
CH = 4096
KLEN = 128
ROWS = 512
WLEN = 256
HOT = 4
WINDOWS = 16
REF = 4096


def shared_routing(key):
    base = jax.random.fold_in(key, 7)
    first, second, third = jax.random.split(base, 3)
    owners = WINDOWS // 2
    ranking = jax.random.permutation(first, WINDOWS).astype(jnp.int32)
    busiest = jax.random.randint(second, (), 0, owners).astype(jnp.int32)
    others = jax.random.permutation(third, owners - 1).astype(jnp.int32)
    others = others + (others >= busiest).astype(jnp.int32)
    position = jnp.clip(ranking - HOT, 0, WINDOWS - HOT - 1) % (owners - 1)
    return jnp.where(ranking < HOT, busiest, others[position]).astype(jnp.int32)


def draw_blocks(key, part):
    return shared_routing(key)


def draw_sites(key, part):
    chosen = shared_routing(key)
    offset = jax.random.randint(jax.random.fold_in(key, 11), (WINDOWS,), ROWS // 4, ROWS).astype(jnp.int32)
    return (chosen * ROWS + offset).astype(jnp.int32)


def draw_filters(key, part):
    first, second = jax.random.split(jax.random.fold_in(key, 3))
    life = jnp.exp(jax.random.uniform(first, (CH, 1), jnp.float32, math.log(30.0), math.log(4000.0)))
    raw = jnp.clip(jax.random.normal(second, (CH, KLEN), jnp.float32), -4.0, 4.0)
    ratio = jnp.exp(-1.0 / life)
    lags = jnp.arange(KLEN, dtype=jnp.float32)[None, :]
    decay = jnp.exp(-lags / life)
    total = (1.0 - ratio ** (2 * KLEN)) / (1.0 - ratio * ratio)
    return (raw * decay / jnp.sqrt(total)).astype(jnp.float32)


def levels(rng, shape, cuts, least, top_value):
    def one(dim, shards_of):
        draws = jax.random.uniform(jax.random.fold_in(jax.random.fold_in(rng, 6), dim), (shards_of,), jnp.float32, least / len(cuts), top_value / len(cuts))
        return jnp.repeat(jnp.exp(draws), shape[dim] // shards_of).reshape((-1,) + (1,) * (len(shape) - dim - 1))

    level = one(*cuts[0])
    for cut in cuts[1:]:
        level = level * one(*cut)
    return level


def centred(rng, extent, width, reach, cuts=(), held_as=jnp.bfloat16):
    array = jax.random.normal(rng, extent, jnp.float32) * width
    if len(cuts) > 0:
        array = levels(rng, extent, cuts, -0.22, 0.18) * array
    return jnp.clip(array, min=-reach, max=reach).astype(held_as)


def setup_inputs(seed: int = 0, part: int = 0) -> dict:
    seeds = jax.random.split(jax.random.key(seed), 9)
    part_splits = jax.random.split(jax.random.fold_in(seeds[8], part), 9)
    return {
        "gate_stream": centred(part_splits[0], (REF, CH), 1.0, 6.0, ((0, 8), (1, 2))),
        "key_stream": centred(part_splits[1], (REF, CH), 1.0, 6.0, ((0, 8), (1, 2))),
        "value_stream": centred(part_splits[2], (REF, CH), 1.0, 6.0, ((0, 8), (1, 2))),
        "filters": draw_filters(jax.random.fold_in(seeds[8], 71), part),
        "temps": jnp.clip(jnp.exp(math.log(24.0) - 1.7917595 * jax.random.uniform(seeds[4], (HEADS,), jnp.float32) ** levels(seeds[4], (HEADS,), ((0, 2),), -0.2, 0.2)), 4.0, 24.0),
        "queries": centred(part_splits[5], (WINDOWS, WLEN, CH), 1.0, 6.0, ((1, 8), (2, 2))),
        "blocks": draw_blocks(jax.random.fold_in(jax.random.fold_in(seeds[8], part), 71), part),
        "sites": draw_sites(jax.random.fold_in(jax.random.fold_in(seeds[8], part), 71), part),
    }


def widen(block):
    return lax.optimization_barrier(block).astype(jnp.float32)

def causal_mix(product, filters):
    taps = filters.shape[1]
    padded = jnp.concatenate([jnp.zeros((taps - 1, CH), jnp.bfloat16), product], 0)
    starts = (jnp.arange(REF // ROWS) * ROWS).astype(jnp.int32)

    def one_block(start):
        piece = widen(lax.dynamic_slice_in_dim(padded, start, ROWS + taps - 1, 0))

        def add_tap(step, total):
            shifted = lax.dynamic_slice_in_dim(piece, (taps - 1 - step).astype(jnp.int32), ROWS, 0)
            column = lax.dynamic_slice_in_dim(filters, step.astype(jnp.int32), 1, 1)[:, 0]
            return total + column[None, :] * shifted
        return lax.fori_loop(0, taps, add_tap, jnp.zeros((ROWS, CH), jnp.float32))
    return lax.map(one_block, starts).reshape(REF, CH)

def head_norm(block):
    shaped = widen(block).reshape(block.shape[:-1] + (HEADS, HEAD_DIM))
    scale = lax.rsqrt(lax.optimization_barrier(jnp.mean(shaped * shaped, axis=-1, keepdims=True)) + 1e-06)
    return (shaped * scale).reshape(block.shape).astype(jnp.bfloat16)

def attend(query_rows, key_rows, value_rows, offset, temps):
    qnorm = widen(head_norm(query_rows)).reshape(WLEN, HEADS, HEAD_DIM)
    keyed = widen(key_rows).reshape(ROWS, HEADS, HEAD_DIM)
    valued = widen(value_rows).reshape(ROWS, HEADS, HEAD_DIM)
    scores = jnp.einsum('qhd,khd->hqk', qnorm, keyed) * (temps / HEAD_DIM)[:, None, None]
    live = jnp.arange(ROWS)[None, None, :] < offset
    weights = jnp.where(live, jnp.exp(scores), 0.0)
    total = lax.optimization_barrier(jnp.sum(weights, axis=-1))
    numer = jnp.einsum('hqk,khd->qhd', widen(weights.astype(jnp.bfloat16)), valued)
    return (numer / total.T[:, :, None]).reshape(WLEN, CH).astype(jnp.bfloat16)

def reference(gate_stream, key_stream, value_stream, filters, temps, queries, blocks, sites):
    product = (key_stream.astype(jnp.float32) * value_stream.astype(jnp.float32)).astype(jnp.bfloat16)
    mixed = causal_mix(product, filters)
    hyena_out = (gate_stream.astype(jnp.float32) * mixed).astype(jnp.bfloat16)
    keys = head_norm(hyena_out)

    def one_window(item):
        query_rows, block, site = item
        start = (block * ROWS).astype(jnp.int32)
        key_rows = lax.dynamic_slice_in_dim(keys, start, ROWS, 0)
        value_rows = lax.dynamic_slice_in_dim(hyena_out, start, ROWS, 0)
        return attend(query_rows, key_rows, value_rows, site - block * ROWS, temps)
    attended = lax.map(one_window, (queries, blocks, sites))
    return (hyena_out, attended)
```

```python
import functools

import jax
import jax.numpy as jnp
import numpy as np
from jax import lax
from jax.experimental import pallas as pl
from jax.experimental.pallas import tpu as pltpu
from jax.sharding import PartitionSpec as P

HEAD_DIM = 128
HOT = 4
EPS = 1e-06
LOG2E = 1.4426950408889634
MIB = 1 << 20


def halves(array):
    high = array.astype(jnp.bfloat16)
    low = (array - high.astype(jnp.float32)).astype(jnp.bfloat16)
    return high, low


def transforms(taps):
    size = 2 * taps
    odd = 2 * np.arange(taps) + 1
    angle = np.pi / size * ((odd[:, None] * np.arange(size)[None, :]) % (2 * size))
    forward = np.concatenate([np.cos(angle), -np.sin(angle)], 0)
    inverse = forward.T[taps:] * (2.0 / size)
    out = []
    for matrix in (forward, inverse):
        high = matrix.astype(jnp.bfloat16)
        low = (matrix - high.astype(np.float64)).astype(jnp.bfloat16)
        out.append(np.concatenate([high, low], 0))
    return out


def unit(block):
    return block * lax.rsqrt(jnp.mean(block * block, axis=-1, keepdims=True) + EPS)


def mix_kernel(gate, key, value, earlier, filters, forward, inverse, out, rows_of, keys_of):
    rows, wide = gate.shape
    taps = filters.shape[1]
    size = 2 * taps
    f32 = jnp.float32
    fwd = forward[...]
    inv = inverse[...]
    high, low = halves(filters[...])
    across = (((1,), (1,)), ((), ()))
    both = lax.dot_general(fwd[:, :taps], high, across, preferred_element_type=f32)
    spectrum = both[:size] + both[size:]
    spectrum += lax.dot_general(fwd[:size, :taps], low, across, preferred_element_type=f32)
    hr, hi = spectrum[:taps], spectrum[taps:]
    before = earlier[...]
    for start in range(0, rows, taps):
        part = slice(start, start + taps)
        now = (key[part, :].astype(f32) * value[part, :].astype(f32)).astype(jnp.bfloat16)
        both = jnp.dot(fwd, jnp.concatenate([before, now], 0), preferred_element_type=f32)
        seen = both[:size] + both[size:]
        xr, xi = seen[:taps], seen[taps:]
        product = jnp.concatenate([xr * hr - xi * hi, xr * hi + xi * hr], 0)
        high, low = halves(product)
        both = jnp.dot(inv, high, preferred_element_type=f32)
        mixed = both[:taps] + both[taps:]
        mixed += jnp.dot(inv[:taps], low, preferred_element_type=f32)
        result = (gate[part, :].astype(f32) * mixed).astype(jnp.bfloat16)
        out[part, :] = result
        for head in range(wide // HEAD_DIM):
            piece = result[:, head * HEAD_DIM : (head + 1) * HEAD_DIM]
            rows_of[head, part, :] = piece
            keys_of[head, part, :] = unit(piece.astype(f32)).astype(jnp.bfloat16)
        before = now


def mix(gate, key, value, earlier, filters):
    rows, chans = gate.shape
    taps = filters.shape[1]
    heads = chans // HEAD_DIM
    wide = 2 * HEAD_DIM
    each = wide // HEAD_DIM
    forward, inverse = (jnp.asarray(matrix) for matrix in transforms(taps))
    stream = pl.BlockSpec((rows, wide), lambda i: (0, i))
    by_head = pl.BlockSpec((each, rows, HEAD_DIM), lambda i: (i, 0, 0))
    whole = lambda array: pl.BlockSpec(array.shape, lambda i: (0, 0))
    per_head = jax.ShapeDtypeStruct((heads, rows, HEAD_DIM), jnp.bfloat16)
    return pl.pallas_call(
        mix_kernel,
        grid=(chans // wide,),
        in_specs=[
            stream,
            stream,
            stream,
            pl.BlockSpec((taps, wide), lambda i: (0, i)),
            pl.BlockSpec((wide, taps), lambda i: (i, 0)),
            whole(forward),
            whole(inverse),
        ],
        out_specs=[stream, by_head, by_head],
        out_shape=[jax.ShapeDtypeStruct((rows, chans), jnp.bfloat16), per_head, per_head],
        compiler_params=pltpu.CompilerParams(vmem_limit_bytes=32 * MIB),
        cost_estimate=pl.CostEstimate(
            flops=16 * rows * taps * chans, bytes_accessed=14 * rows * chans, transcendentals=0
        ),
        name="mix",
    )(gate, key, value, earlier, filters, forward, inverse)


def softened(query, keys, rows, heat, live):
    f32 = jnp.float32
    query = unit(query).astype(jnp.bfloat16)
    scores = lax.dot_general(query, keys, (((1,), (1,)), ((), ())), preferred_element_type=f32)
    weights = jnp.where(live, jnp.exp2(scores * heat), 0.0)
    total = jnp.sum(weights, axis=-1, keepdims=True)
    return jnp.dot(weights.astype(jnp.bfloat16), rows, preferred_element_type=f32) / total


def masks(offsets, first, slots, tokens, positions):
    place = lax.broadcasted_iota(jnp.int32, (tokens, positions), 1)
    return jnp.concatenate([place < offsets[first + slot] for slot in range(slots)], 0)


def attend_kernel(offsets, temps, queries, keys, rows, out):
    slots, tokens, wide = queries.shape
    f32 = jnp.float32
    live = masks(offsets, 0, slots, tokens, keys.shape[1])
    each = wide // HEAD_DIM
    base = pl.program_id(0) * each
    for head in range(each):
        cols = slice(head * HEAD_DIM, (head + 1) * HEAD_DIM)
        query = queries[:, :, cols].astype(f32).reshape(slots * tokens, HEAD_DIM)
        heat = temps[base + head] * (LOG2E / HEAD_DIM)
        done = softened(query, keys[head], rows[head], heat, live)
        out[:, :, cols] = done.reshape(slots, tokens, HEAD_DIM).astype(jnp.bfloat16)


def attend(offsets, temps, message, keys, rows):
    heads, positions, _ = keys.shape
    slots, tokens, _ = message.shape
    each = 4
    wide = each * HEAD_DIM
    scalars = pl.BlockSpec(memory_space=pltpu.SMEM)
    block = pl.BlockSpec((slots, tokens, wide), lambda i: (0, 0, i))
    by_head = pl.BlockSpec((each, positions, HEAD_DIM), lambda i: (i, 0, 0))
    work = slots * tokens * positions * heads
    return pl.pallas_call(
        attend_kernel,
        grid=(heads // each,),
        in_specs=[scalars, scalars, block, by_head, by_head],
        out_specs=block,
        out_shape=jax.ShapeDtypeStruct((slots, tokens, heads * HEAD_DIM), jnp.bfloat16),
        compiler_params=pltpu.CompilerParams(vmem_limit_bytes=24 * MIB),
        cost_estimate=pl.CostEstimate(
            flops=4 * work * HEAD_DIM, bytes_accessed=4 * keys.size, transcendentals=work
        ),
        name="attend",
    )(offsets, temps, message, keys, rows)


def extra_kernel(offsets, temps, place, rows, *refs):
    queries, out = refs[:-1], refs[-1]
    extras, tokens, wide = queries[0].shape
    f32 = jnp.float32
    me = place[0]
    live = masks(offsets, 0, extras, tokens, rows.shape[1])
    for head in range(wide // HEAD_DIM):
        cols = slice(head * HEAD_DIM, (head + 1) * HEAD_DIM)
        valued = rows[head]
        keyed = unit(valued.astype(f32)).astype(jnp.bfloat16)
        heat = temps[place[1] * (wide // HEAD_DIM) + head] * (LOG2E / HEAD_DIM)
        for step, source in enumerate(queries):
            query = source[:, :, cols].astype(f32).reshape(extras * tokens, HEAD_DIM)
            done = softened(query, keyed, valued, heat, live)
            done = done.reshape(1, extras, tokens, HEAD_DIM).astype(jnp.bfloat16)
            out[pl.ds(jnp.bitwise_xor(me, step), 1), :, :, cols] = done


def attend_extra(offsets, temps, place, rows, messages, chans):
    peers = len(messages)
    extras, tokens, _ = messages[0].shape
    wide = chans // peers
    scalars = pl.BlockSpec(memory_space=pltpu.SMEM)
    positions = rows.shape[1]
    work = extras * tokens * positions * peers * wide // HEAD_DIM
    return pl.pallas_call(
        extra_kernel,
        grid=(1,),
        in_specs=[scalars, scalars, scalars, pl.BlockSpec(rows.shape, lambda i: (0, 0, 0))]
        + [pl.BlockSpec((extras, tokens, wide), lambda i: (0, 0, chans // wide))] * peers,
        out_specs=pl.BlockSpec((peers, extras, tokens, wide), lambda i: (0, 0, 0, 0)),
        out_shape=jax.ShapeDtypeStruct((peers, extras, tokens, wide), jnp.bfloat16),
        compiler_params=pltpu.CompilerParams(vmem_limit_bytes=24 * MIB),
        cost_estimate=pl.CostEstimate(
            flops=4 * work * HEAD_DIM, bytes_accessed=2 * MIB, transcendentals=work
        ),
        name="attend_extra",
    )(offsets, temps, place, rows, *messages)


def mirrored(index, peers):
    result = 0
    for bit in range(peers.bit_length() - 1):
        result = result * 2 + jnp.bitwise_and(lax.shift_right_logical(index, bit), 1)
    return result


def pack_kernel(slots, place, table, queries, *refs):
    outs, sems = refs[:-1], refs[-1]
    peers = len(outs)
    chans = queries.shape[2]
    wide = outs[0].shape[2] - chans
    extras = HOT - slots if wide else 0
    copies = []
    for step, out in enumerate(outs):
        peer = jnp.bitwise_xor(place[0], step)
        for slot in range(slots):
            window = jnp.maximum(table[peer * HOT + slot], 0)
            target = out.at[slot, :, pl.ds(0, chans)] if wide else out.at[slot]
            copies.append((queries.at[window], target))
        if extras:
            start = pl.multiple_of(mirrored(peer, peers) * wide, wide)
        for extra in range(extras):
            window = table[place[2] * HOT + slots + extra]
            copies.append(
                (queries.at[window, :, pl.ds(start, wide)], out.at[extra, :, pl.ds(chans, wide)])
            )
    copies = [pltpu.make_async_copy(*pair, sems.at[i]) for i, pair in enumerate(copies)]
    for copy in copies:
        copy.start()
    for copy in copies:
        copy.wait()


def pack(place, table, queries, peers, slots, wide):
    _, tokens, chans = queries.shape
    scalars = pl.BlockSpec(memory_space=pltpu.SMEM)
    anywhere = pl.BlockSpec(memory_space=pl.ANY)
    extras = HOT - slots if wide else 0
    return pl.pallas_call(
        functools.partial(pack_kernel, slots),
        in_specs=[scalars, scalars, anywhere],
        out_specs=[anywhere] * peers,
        out_shape=[jax.ShapeDtypeStruct((slots, tokens, chans + wide), queries.dtype)] * peers,
        scratch_shapes=[pltpu.SemaphoreType.DMA((peers * (slots + extras),))],
        name="pack",
    )(place, table, queries)


def unpack_kernel(slots, peers, place, table, *refs):
    results, extra_results = refs[:peers], refs[peers:-2]
    out, sems = refs[-2:]
    copies = []
    for step, source in enumerate(results):
        peer = jnp.bitwise_xor(place[0], step)
        for slot in range(slots):
            window = table[peer * HOT + slot]
            copies.append((window, source.at[slot], out.at[jnp.maximum(window, 0)]))
    for source in extra_results:
        _, extras, _, wide = source.shape
        for peer in range(peers):
            start = pl.multiple_of(mirrored(jnp.int32(peer), peers) * wide, wide)
            for extra in range(extras):
                window = table[place[2] * HOT + slots + extra]
                target = out.at[jnp.maximum(window, 0), :, pl.ds(start, wide)]
                copies.append((window, source.at[peer, extra], target))

    def each(act):
        for i, (window, source, target) in enumerate(copies):
            copy = pltpu.make_async_copy(source, target, sems.at[i])
            pl.when(window >= 0)(functools.partial(act, copy))

    each(lambda copy: copy.start())
    each(lambda copy: copy.wait())


def unpack(place, table, results, extra_results, windows):
    peers = len(results)
    slots, tokens, chans = results[0].shape
    scalars = pl.BlockSpec(memory_space=pltpu.SMEM)
    anywhere = pl.BlockSpec(memory_space=pl.ANY)
    count = peers * slots + sum(array.shape[0] * array.shape[1] for array in extra_results)
    return pl.pallas_call(
        functools.partial(unpack_kernel, slots, peers),
        in_specs=[scalars, scalars] + [anywhere] * (peers + len(extra_results)),
        out_specs=anywhere,
        out_shape=jax.ShapeDtypeStruct((windows, tokens, chans), results[0].dtype),
        scratch_shapes=[pltpu.SemaphoreType.DMA((count,))],
        name="unpack",
    )(place, table, *results, *extra_results)


def exchanged(value, step):
    peers = lax.axis_size("pos")
    if step == 0:
        return value
    return lax.ppermute(value, "pos", [(i, i ^ step) for i in range(peers)])


def spread(rows, me, hot, peers):
    held = rows
    for bit in range(peers.bit_length() - 1):
        count = held.shape[0] // 2
        mine = jnp.bitwise_and(lax.shift_right_logical(me, bit), 1)
        sent = lax.dynamic_slice_in_dim(held, (1 - mine) * count, count, 0)
        kept = lax.dynamic_slice_in_dim(held, mine * count, count, 0)
        arrived = exchanged(sent, 1 << bit)
        have = lax.shift_right_logical(me, bit) == lax.shift_right_logical(hot, bit)
        held = jnp.where(have, kept, arrived)
    return held


def shards(gate_stream, key_stream, value_stream, filters, temps, queries, blocks, sites):
    rows, chans = gate_stream.shape
    taps = filters.shape[1]
    peers = lax.axis_size("pos")
    me = lax.axis_index("pos").astype(jnp.int32)
    windows = blocks.shape[0]
    heads = chans // HEAD_DIM
    extras = 2 if heads % peers == 0 else 0
    slots = HOT - extras
    wide = chans // peers if extras else 0

    last = slice(rows - taps, rows)
    product = key_stream[last].astype(jnp.float32) * value_stream[last].astype(jnp.float32)
    earlier = lax.ppermute(
        product.astype(jnp.bfloat16), "pos", [(i, i + 1) for i in range(peers - 1)]
    )

    order = jnp.arange(windows)
    same = (blocks[:, None] == blocks[None, :]) & (order[None, :] < order[:, None])
    within = jnp.sum(same, axis=1)
    hot = jnp.sum(jnp.where(within == HOT - 1, blocks, 0))
    named = jnp.arange(peers * HOT)[:, None] == (blocks * HOT + within)[None, :]
    table = (jnp.sum(jnp.where(named, order[None, :] + 1, 0), axis=1) - 1).astype(jnp.int32)
    offset = jnp.sum(jnp.where(named, (sites - blocks * rows)[None, :], 0), axis=1)
    offset = jnp.where(table >= 0, offset, rows).astype(jnp.int32)
    mine = lax.dynamic_slice_in_dim(offset, me * HOT, HOT, 0)
    place = jnp.stack([me, mirrored(me, peers), hot]).astype(jnp.int32)

    messages = pack(place, table, queries, peers, slots, wide)
    arrived = [exchanged(message, step) for step, message in enumerate(messages)]
    hyena_out, valued, keyed = mix(gate_stream, key_stream, value_stream, earlier, filters)
    results = [attend(mine, temps, message, keyed, valued) for message in arrived]
    returned = [exchanged(result, step) for step, result in enumerate(results)]
    extra_results = []
    if extras:
        share = spread(valued, me, hot, peers)
        theirs = lax.dynamic_slice_in_dim(offset, hot * HOT + slots, extras, 0)
        result = attend_extra(theirs, temps, place, share, arrived, chans)
        extra_results.append(lax.all_to_all(result, "pos", 0, 0, tiled=True))
    attended = unpack(place, table, returned, extra_results, windows)
    return (hyena_out, attended)


def solution(mesh):
    placed = (
        P(("groups", "pos"), "mp"),
        P(("groups", "pos"), "mp"),
        P(("groups", "pos"), "mp"),
        P("mp", None),
        P("mp"),
        P("groups", "pos", "mp"),
        P("groups"),
        P("groups"),
    )
    return jax.shard_map(
        shards,
        mesh=mesh,
        in_specs=placed,
        out_specs=(P(("groups", "pos"), "mp"), P("groups", "pos", "mp")),
        check_vma=False,
    )
```

```python
import functools

import jax
import jax.numpy as jnp
import numpy as np
from jax import lax
from jax.experimental import pallas as pl
from jax.experimental.pallas import tpu as pltpu
from jax.sharding import PartitionSpec as P

HEAD_DIM = 128
HOT = 4
EPS = 1e-06
LOG2E = 1.4426950408889634
MIB = 1 << 20
AHEAD = 16
SMALL = pl.CostEstimate(flops=1000, bytes_accessed=1000, transcendentals=0)


def halves(array):
    high = array.astype(jnp.bfloat16)
    low = (array - high.astype(jnp.float32)).astype(jnp.bfloat16)
    return high, low


def transforms(taps):
    size = 2 * taps
    odd = 2 * np.arange(taps) + 1
    angle = np.pi / size * ((odd[:, None] * np.arange(size)[None, :]) % (2 * size))
    forward = np.concatenate([np.cos(angle), -np.sin(angle)], 0)
    inverse = forward.T[taps:] * (2.0 / size)
    out = []
    for matrix in (forward, inverse):
        high = matrix.astype(jnp.bfloat16)
        low = (matrix - high.astype(np.float64)).astype(jnp.bfloat16)
        out.append(np.concatenate([high, low], 0))
    return out


def unit(block):
    return block * lax.rsqrt(jnp.mean(block * block, axis=-1, keepdims=True) + EPS)


def mix_kernel(gate, key, value, earlier, filters, forward, inverse, out, rows_of, keys_of):
    rows, wide = gate.shape
    taps = filters.shape[1]
    size = 2 * taps
    f32 = jnp.float32
    fwd = forward[...]
    inv = inverse[...]
    high, low = halves(filters[...])
    across = (((1,), (1,)), ((), ()))
    both = lax.dot_general(fwd[:, :taps], high, across, preferred_element_type=f32)
    spectrum = both[:size] + both[size:]
    spectrum += lax.dot_general(fwd[:size, :taps], low, across, preferred_element_type=f32)
    hr, hi = spectrum[:taps], spectrum[taps:]
    before = earlier[...]
    for start in range(0, rows, taps):
        part = slice(start, start + taps)
        now = (key[part, :].astype(f32) * value[part, :].astype(f32)).astype(jnp.bfloat16)
        both = jnp.dot(fwd, jnp.concatenate([before, now], 0), preferred_element_type=f32)
        seen = both[:size] + both[size:]
        xr, xi = seen[:taps], seen[taps:]
        product = jnp.concatenate([xr * hr - xi * hi, xr * hi + xi * hr], 0)
        high, low = halves(product)
        both = jnp.dot(inv, high, preferred_element_type=f32)
        mixed = both[:taps] + both[taps:]
        mixed += jnp.dot(inv[:taps], low, preferred_element_type=f32)
        result = (gate[part, :].astype(f32) * mixed).astype(jnp.bfloat16)
        out[part, :] = result
        for head in range(wide // HEAD_DIM):
            piece = result[:, head * HEAD_DIM : (head + 1) * HEAD_DIM]
            rows_of[head, part, :] = piece
            keys_of[head, :, part] = unit(piece.astype(f32)).astype(jnp.bfloat16).T
        before = now


def mix(gate, key, value, earlier, filters):
    rows, chans = gate.shape
    taps = filters.shape[1]
    heads = chans // HEAD_DIM
    wide = 2 * HEAD_DIM
    each = wide // HEAD_DIM
    forward, inverse = (jnp.asarray(matrix) for matrix in transforms(taps))
    stream = pl.BlockSpec((rows, wide), lambda i: (0, i))
    by_head = pl.BlockSpec((each, rows, HEAD_DIM), lambda i: (i, 0, 0))
    whole = lambda array: pl.BlockSpec(array.shape, lambda i: (0, 0))
    turned = pl.BlockSpec((each, HEAD_DIM, rows), lambda i: (i, 0, 0))
    per_head = jax.ShapeDtypeStruct((heads, rows, HEAD_DIM), jnp.bfloat16)
    per_head_turned = jax.ShapeDtypeStruct((heads, HEAD_DIM, rows), jnp.bfloat16)
    return pl.pallas_call(
        mix_kernel,
        grid=(chans // wide,),
        in_specs=[
            stream,
            stream,
            stream,
            pl.BlockSpec((taps, wide), lambda i: (0, i)),
            pl.BlockSpec((wide, taps), lambda i: (i, 0)),
            whole(forward),
            whole(inverse),
        ],
        out_specs=[stream, by_head, turned],
        out_shape=[jax.ShapeDtypeStruct((rows, chans), jnp.bfloat16), per_head, per_head_turned],
        compiler_params=pltpu.CompilerParams(vmem_limit_bytes=32 * MIB),
        cost_estimate=SMALL,
        name="mix",
    )(gate, key, value, earlier, filters, forward, inverse)


def softened(query, keys, rows, heat, live):
    f32 = jnp.float32
    query = unit(query).astype(jnp.bfloat16)
    scores = jnp.dot(query, keys, preferred_element_type=f32)
    weights = jnp.where(live, jnp.exp2(scores * heat), 0.0)
    total = jnp.sum(weights, axis=-1, keepdims=True)
    return jnp.dot(weights.astype(jnp.bfloat16), rows, preferred_element_type=f32) / total


def masks(offsets, first, slots, tokens, positions):
    place = lax.broadcasted_iota(jnp.int32, (tokens, positions), 1)
    return jnp.concatenate([place < offsets[first + slot] for slot in range(slots)], 0)


def attend_kernel(info, temps, queries, keys, rows, out):
    slots, tokens, _ = queries.shape
    heads, _, positions = keys.shape
    live = masks(info, info.shape[0] - AHEAD, slots, tokens, positions)

    def one(head, carry):
        cols = pl.ds(pl.multiple_of(head * HEAD_DIM, HEAD_DIM), HEAD_DIM)
        query = queries[:, :, cols].astype(jnp.float32).reshape(slots * tokens, HEAD_DIM)
        heat = temps[head] * (LOG2E / HEAD_DIM)
        done = softened(query, keys[head], rows[head], heat, live)
        out[:, :, cols] = done.reshape(slots, tokens, HEAD_DIM).astype(jnp.bfloat16)
        return carry

    lax.fori_loop(0, heads, one, 0, unroll=4)


def attend(info, temps, message, keys, rows):
    heads, positions, _ = rows.shape
    slots, tokens, _ = message.shape
    scalars = pl.BlockSpec(memory_space=pltpu.SMEM)
    vector = pl.BlockSpec(memory_space=pltpu.VMEM)
    return pl.pallas_call(
        attend_kernel,
        in_specs=[scalars, scalars, vector, vector, vector],
        out_specs=vector,
        out_shape=jax.ShapeDtypeStruct((slots, tokens, heads * HEAD_DIM), jnp.bfloat16),
        compiler_params=pltpu.CompilerParams(vmem_limit_bytes=24 * MIB),
        cost_estimate=SMALL,
        name="attend",
    )(info, temps, message, keys, rows)


def extra_kernel(info, temps, rows, *refs):
    queries, out = refs[:-1], refs[-1]
    extras, tokens, wide = queries[0].shape
    me = lax.axis_index("pos")
    share = mirrored(me, len(queries)) * (wide // HEAD_DIM)
    live = masks(info, info.shape[0] - AHEAD + HOT, extras, tokens, rows.shape[1])
    for head in range(wide // HEAD_DIM):
        cols = slice(head * HEAD_DIM, (head + 1) * HEAD_DIM)
        valued = rows[head]
        keyed = unit(valued.astype(jnp.float32)).astype(jnp.bfloat16).T
        heat = temps[share + head] * (LOG2E / HEAD_DIM)
        for step, source in enumerate(queries):
            query = source[:, :, cols].astype(jnp.float32).reshape(extras * tokens, HEAD_DIM)
            done = softened(query, keyed, valued, heat, live)
            done = done.reshape(1, extras, tokens, HEAD_DIM).astype(jnp.bfloat16)
            out[pl.ds(jnp.bitwise_xor(me, step), 1), :, :, cols] = done


def attend_extra(info, temps, rows, messages, chans):
    peers = len(messages)
    extras, tokens, _ = messages[0].shape
    wide = chans // peers
    scalars = pl.BlockSpec(memory_space=pltpu.SMEM)
    return pl.pallas_call(
        extra_kernel,
        grid=(1,),
        in_specs=[scalars, scalars, pl.BlockSpec(rows.shape, lambda i: (0, 0, 0))]
        + [pl.BlockSpec((extras, tokens, wide), lambda i: (0, 0, chans // wide))] * peers,
        out_specs=pl.BlockSpec((peers, extras, tokens, wide), lambda i: (0, 0, 0, 0)),
        out_shape=jax.ShapeDtypeStruct((peers, extras, tokens, wide), jnp.bfloat16),
        compiler_params=pltpu.CompilerParams(vmem_limit_bytes=24 * MIB),
        cost_estimate=SMALL,
        name="attend_extra",
    )(info, temps, rows, *messages)


def mirrored_number(index, peers):
    bits = peers.bit_length() - 1
    return sum(((index >> bit) & 1) << (bits - 1 - bit) for bit in range(bits))


def mirrored(index, peers):
    result = jnp.int32(0)
    for bit in range(peers.bit_length() - 1):
        result = result * 2 + jnp.bitwise_and(lax.shift_right_logical(index, bit), 1)
    return result


def pack_kernel(slots, rows, blocks, sites, queries, key, value, info, tail, *outs):
    peers = len(outs)
    windows, _, chans = queries.shape
    wide = outs[0].shape[2] - chans
    extras = HOT - slots if wide else 0
    me = lax.axis_index("pos")
    ahead = info.shape[0] - AHEAD
    hot_at = info.shape[0] - 1

    def clear(at, carry):
        info[at] = -1
        return carry

    lax.fori_loop(0, info.shape[0], clear, 0)
    for window in range(windows):
        block = blocks[window]
        count = jnp.int32(0)
        for slot in range(HOT - 1):
            count += (info[block * HOT + slot] >= 0).astype(jnp.int32)
        info[block * HOT + count] = window

        @pl.when(count == HOT - 1)
        def _():
            info[hot_at] = block

    hot = info[hot_at]

    def offset(entry):
        window = info[entry]
        site = sites[jnp.maximum(window, 0)]
        return jnp.where(window >= 0, site - rows * (entry // HOT), rows)

    for slot in range(HOT):
        info[ahead + slot] = offset(me * HOT + slot)
    for extra in range(extras):
        info[ahead + HOT + extra] = offset(hot * HOT + slots + extra)

    tail[...] = (key[...].astype(jnp.float32) * value[...].astype(jnp.float32)).astype(jnp.bfloat16)
    for step, out in enumerate(outs):
        peer = jnp.bitwise_xor(me, step)
        for slot in range(slots):
            window = jnp.maximum(info[peer * HOT + slot], 0)
            out[slot, :, :chans] = queries[window]
        if extras:
            start = pl.multiple_of(mirrored(peer, peers) * wide, wide)
        for extra in range(extras):
            window = info[hot * HOT + slots + extra]
            out[extra, :, chans:] = queries[window, :, pl.ds(start, wide)]


def pack(blocks, sites, queries, key, value, taps, peers, slots, wide):
    _, tokens, chans = queries.shape
    rows = key.shape[0]
    scalars = pl.BlockSpec(memory_space=pltpu.SMEM)
    vector = pl.BlockSpec(memory_space=pltpu.VMEM)
    last = pl.BlockSpec((taps, chans), lambda i: (rows // taps - 1, 0))
    whole = pl.BlockSpec(queries.shape, lambda i: (0, 0, 0))
    message = jax.ShapeDtypeStruct((slots, tokens, chans + wide), queries.dtype)
    info, tail, *messages = pl.pallas_call(
        functools.partial(pack_kernel, slots, rows),
        grid=(1,),
        in_specs=[scalars, scalars, whole, last, last],
        out_specs=[scalars, vector] + [vector] * peers,
        out_shape=[
            jax.ShapeDtypeStruct((peers * HOT + AHEAD,), jnp.int32),
            jax.ShapeDtypeStruct((taps, chans), jnp.bfloat16),
        ]
        + [message] * peers,
        compiler_params=pltpu.CompilerParams(vmem_limit_bytes=24 * MIB),
        cost_estimate=SMALL,
        name="pack",
    )(blocks, sites, queries, key, value)
    return info, tail, messages


def unpack_kernel(slots, peers, info, *refs):
    results, extra_results, out = refs[:peers], refs[peers:-1], refs[-1]
    me = lax.axis_index("pos")
    hot = info[info.shape[0] - 1]
    for step, source in enumerate(results):
        peer = jnp.bitwise_xor(me, step)
        for slot in range(slots):
            window = info[peer * HOT + slot]

            @pl.when(window >= 0)
            def _():
                out[pl.ds(window, 1)] = source[slot : slot + 1]

    for source in extra_results:
        _, extras, _, wide = source.shape
        for extra in range(extras):
            window = info[hot * HOT + slots + extra]
            for peer in range(peers):
                start = int(mirrored_number(peer, peers)) * wide
                out[pl.ds(window, 1), :, start : start + wide] = source[peer, extra : extra + 1]


def unpack(info, results, extra_results, windows):
    peers = len(results)
    slots, tokens, chans = results[0].shape
    scalars = pl.BlockSpec(memory_space=pltpu.SMEM)
    vector = pl.BlockSpec(memory_space=pltpu.VMEM)
    return pl.pallas_call(
        functools.partial(unpack_kernel, slots, peers),
        in_specs=[scalars] + [vector] * (peers + len(extra_results)),
        out_specs=vector,
        out_shape=jax.ShapeDtypeStruct((windows, tokens, chans), results[0].dtype),
        compiler_params=pltpu.CompilerParams(vmem_limit_bytes=24 * MIB),
        cost_estimate=SMALL,
        name="unpack",
    )(info, *results, *extra_results)


def exchanged(value, step):
    peers = lax.axis_size("pos")
    if step == 0:
        return value
    return lax.ppermute(value, "pos", [(i, i ^ step) for i in range(peers)])


def spread(rows, me, hot, peers):
    held = rows
    for bit in range(peers.bit_length() - 1):
        count = held.shape[0] // 2
        mine = jnp.bitwise_and(lax.shift_right_logical(me, bit), 1)
        sent = lax.dynamic_slice_in_dim(held, (1 - mine) * count, count, 0)
        kept = lax.dynamic_slice_in_dim(held, mine * count, count, 0)
        arrived = exchanged(sent, 1 << bit)
        have = lax.shift_right_logical(me, bit) == lax.shift_right_logical(hot, bit)
        held = jnp.where(have, kept, arrived)
    return held


def shards(gate_stream, key_stream, value_stream, filters, temps, queries, blocks, sites):
    rows, chans = gate_stream.shape
    taps = filters.shape[1]
    peers = lax.axis_size("pos")
    me = lax.axis_index("pos").astype(jnp.int32)
    windows = blocks.shape[0]
    heads = chans // HEAD_DIM
    extras = 2 if heads % peers == 0 else 0
    slots = HOT - extras
    wide = chans // peers if extras else 0

    info, tail, messages = pack(
        blocks, sites, queries, key_stream, value_stream, taps, peers, slots, wide
    )
    earlier = lax.ppermute(tail, "pos", [(i, i + 1) for i in range(peers - 1)])
    arrived = [exchanged(message, step) for step, message in enumerate(messages)]
    hyena_out, valued, keyed = mix(gate_stream, key_stream, value_stream, earlier, filters)
    results = [attend(info, temps, message, keyed, valued) for message in arrived]
    returned = [exchanged(result, step) for step, result in enumerate(results)]
    extra_results = []
    if extras:
        share = spread(valued, me, info[-1], peers)
        result = attend_extra(info, temps, share, arrived, chans)
        extra_results.append(lax.all_to_all(result, "pos", 0, 0, tiled=True))
    attended = unpack(info, returned, extra_results, windows)
    return (hyena_out, attended)


def solution(mesh):
    placed = (
        P(("groups", "pos"), "mp"),
        P(("groups", "pos"), "mp"),
        P(("groups", "pos"), "mp"),
        P("mp", None),
        P("mp"),
        P("groups", "pos", "mp"),
        P("groups"),
        P("groups"),
    )
    return jax.shard_map(
        shards,
        mesh=mesh,
        in_specs=placed,
        out_specs=(P(("groups", "pos"), "mp"), P("groups", "pos", "mp")),
        check_vma=False,
    )
```

```python
import functools

import jax
import jax.numpy as jnp
import numpy as np
from jax import lax
from jax.experimental import pallas as pl
from jax.experimental.pallas import tpu as pltpu
from jax.sharding import PartitionSpec as P

HEAD_DIM = 128
HOT = 4
EPS = 1e-06
LOG2E = 1.4426950408889634
MIB = 1 << 20
AHEAD = 16
CUT_FLOPS = 2 << 30
ATTEND_FLOPS = 20 << 30
MIX_FLOPS = 100 << 30
PACK_FLOPS = 20 << 30


def cost(flops):
    return pl.CostEstimate(flops=flops, bytes_accessed=1000, transcendentals=0)


def halves(array):
    high = array.astype(jnp.bfloat16)
    low = (array - high.astype(jnp.float32)).astype(jnp.bfloat16)
    return high, low


def transforms(taps):
    size = 2 * taps
    odd = 2 * np.arange(taps) + 1
    angle = np.pi / size * ((odd[:, None] * np.arange(size)[None, :]) % (2 * size))
    forward = np.concatenate([np.cos(angle), -np.sin(angle)], 0)
    inverse = forward.T[taps:] * (2.0 / size)
    out = []
    for matrix in (forward, inverse):
        high = matrix.astype(jnp.bfloat16)
        low = (matrix - high.astype(np.float64)).astype(jnp.bfloat16)
        out.append(np.concatenate([high, low], 0))
    return out


def unit(block):
    return block * lax.rsqrt(jnp.mean(block * block, axis=-1, keepdims=True) + EPS)


def mix_kernel(gate, key, value, earlier, filters, forward, inverse, out, rows_of, keys_of):
    rows, wide = gate.shape
    taps = filters.shape[1]
    size = 2 * taps
    f32 = jnp.float32
    fwd = forward[...]
    inv = inverse[...]
    high, low = halves(filters[...])
    across = (((1,), (1,)), ((), ()))
    both = lax.dot_general(fwd[:, :taps], high, across, preferred_element_type=f32)
    spectrum = both[:size] + both[size:]
    spectrum += lax.dot_general(fwd[:size, :taps], low, across, preferred_element_type=f32)
    hr, hi = spectrum[:taps], spectrum[taps:]
    before = earlier[...]
    for start in range(0, rows, taps):
        part = slice(start, start + taps)
        now = (key[part, :].astype(f32) * value[part, :].astype(f32)).astype(jnp.bfloat16)
        both = jnp.dot(fwd, jnp.concatenate([before, now], 0), preferred_element_type=f32)
        seen = both[:size] + both[size:]
        xr, xi = seen[:taps], seen[taps:]
        product = jnp.concatenate([xr * hr - xi * hi, xr * hi + xi * hr], 0)
        high, low = halves(product)
        both = jnp.dot(inv, high, preferred_element_type=f32)
        mixed = both[:taps] + both[taps:]
        mixed += jnp.dot(inv[:taps], low, preferred_element_type=f32)
        result = (gate[part, :].astype(f32) * mixed).astype(jnp.bfloat16)
        out[part, :] = result
        for head in range(wide // HEAD_DIM):
            piece = result[:, head * HEAD_DIM : (head + 1) * HEAD_DIM]
            rows_of[head, part, :] = piece
            keys_of[head, :, part] = unit(piece.astype(f32)).astype(jnp.bfloat16).T
        before = now


def mix(gate, key, value, earlier, filters):
    rows, chans = gate.shape
    taps = filters.shape[1]
    heads = chans // HEAD_DIM
    wide = 2 * HEAD_DIM
    each = wide // HEAD_DIM
    forward, inverse = (jnp.asarray(matrix) for matrix in transforms(taps))
    stream = pl.BlockSpec((rows, wide), lambda i: (0, i))
    by_head = pl.BlockSpec((each, rows, HEAD_DIM), lambda i: (i, 0, 0))
    whole = lambda array: pl.BlockSpec(array.shape, lambda i: (0, 0))
    turned = pl.BlockSpec((each, HEAD_DIM, rows), lambda i: (i, 0, 0))
    per_head = jax.ShapeDtypeStruct((heads, rows, HEAD_DIM), jnp.bfloat16)
    per_head_turned = jax.ShapeDtypeStruct((heads, HEAD_DIM, rows), jnp.bfloat16)
    return pl.pallas_call(
        mix_kernel,
        grid=(chans // wide,),
        in_specs=[
            stream,
            stream,
            stream,
            pl.BlockSpec((taps, wide), lambda i: (0, i)),
            pl.BlockSpec((wide, taps), lambda i: (i, 0)),
            whole(forward),
            whole(inverse),
        ],
        out_specs=[stream, by_head, turned],
        out_shape=[jax.ShapeDtypeStruct((rows, chans), jnp.bfloat16), per_head, per_head_turned],
        compiler_params=pltpu.CompilerParams(vmem_limit_bytes=48 * MIB),
        cost_estimate=cost(MIX_FLOPS),
        name="mix",
    )(gate, key, value, earlier, filters, forward, inverse)


def softened(query, keys, rows, heat, live):
    f32 = jnp.float32
    query = unit(query).astype(jnp.bfloat16)
    scores = jnp.dot(query, keys, preferred_element_type=f32)
    weights = jnp.where(live, jnp.exp2(scores * heat), 0.0)
    total = jnp.sum(weights, axis=-1, keepdims=True)
    return jnp.dot(weights.astype(jnp.bfloat16), rows, preferred_element_type=f32) / total


def masks(offsets, first, slots, tokens, positions):
    place = lax.broadcasted_iota(jnp.int32, (tokens, positions), 1)
    return jnp.concatenate([place < offsets[first + slot] for slot in range(slots)], 0)


def attend_kernel(count, info, temps, keys, rows, _, *refs):
    sources, outs = refs[:count], refs[count:]
    heads, _, positions = keys.shape
    slots, tokens, _ = sources[0].shape[-3:]
    places = []
    for source, out in zip(sources, outs):
        whole = len(source.shape) == 3
        places += [(source, out, () if whole else (at,)) for at in range(1 if whole else source.shape[0])]
    each = slots * tokens
    live = masks(info, info.shape[0] - AHEAD, slots, tokens, positions)
    live = jnp.concatenate([live] * len(places), 0)
    every = (slice(None), slice(None))

    def one(head, carry):
        cols = pl.ds(pl.multiple_of(head * HEAD_DIM, HEAD_DIM), HEAD_DIM)
        query = [source[at + every + (cols,)].astype(jnp.float32) for source, _, at in places]
        query = [part.reshape(each, HEAD_DIM) for part in query]
        heat = temps[head] * (LOG2E / HEAD_DIM)
        done = softened(jnp.concatenate(query, 0), keys[head], rows[head], heat, live)
        for place, (_, out, at) in enumerate(places):
            part = done[place * each : (place + 1) * each].reshape(slots, tokens, HEAD_DIM)
            out[at + every + (cols,)] = part.astype(jnp.bfloat16)
        return carry

    lax.fori_loop(0, heads, one, 0, unroll=4 if len(places) <= 4 else 1)


def attend(info, temps, keys, rows, after, messages):
    chans = rows.shape[0] * HEAD_DIM
    scalars = pl.BlockSpec(memory_space=pltpu.SMEM)
    vector = pl.BlockSpec(memory_space=pltpu.VMEM)
    anywhere = pl.BlockSpec(memory_space=pl.ANY)
    return pl.pallas_call(
        functools.partial(attend_kernel, len(messages)),
        in_specs=[scalars, scalars, vector, vector, anywhere] + [vector] * len(messages),
        out_specs=[vector] * len(messages),
        out_shape=[
            jax.ShapeDtypeStruct(message.shape[:-1] + (chans,), jnp.bfloat16)
            for message in messages
        ],
        compiler_params=pltpu.CompilerParams(vmem_limit_bytes=16 * MIB),
        cost_estimate=cost(ATTEND_FLOPS),
        name="attend",
    )(info, temps, keys, rows, after, *messages)


def cut_kernel(bit, info, held, *refs):
    sent, kept = refs[-2:]
    me = lax.axis_index("pos")
    count = sent.shape[0]
    mine = jnp.bitwise_and(lax.shift_right_logical(me, bit), 1)
    if bit:
        hot = info[info.shape[0] - 1]
        before = bit - 1
        have = lax.shift_right_logical(me, before) == lax.shift_right_logical(hot, before)
        arrived = refs[0]

        @pl.when(have)
        def _():
            sent[...] = held[pl.ds((1 - mine) * count, count)]
            kept[...] = held[pl.ds(mine * count, count)]

        @pl.when(jnp.logical_not(have))
        def _():
            sent[...] = arrived[pl.ds((1 - mine) * count, count)]
            kept[...] = arrived[pl.ds(mine * count, count)]
    else:
        sent[...] = held[pl.ds((1 - mine) * count, count)]
        kept[...] = held[pl.ds(mine * count, count)]


def cut(bit, info, held, arrived, after):
    count, positions, wide = held.shape
    half = jax.ShapeDtypeStruct((count // 2, positions, wide), held.dtype)
    vector = pl.BlockSpec(memory_space=pltpu.VMEM)
    return pl.pallas_call(
        functools.partial(cut_kernel, bit),
        in_specs=[pl.BlockSpec(memory_space=pltpu.SMEM), vector]
        + [vector] * len(arrived)
        + [pl.BlockSpec(memory_space=pl.ANY)],
        out_specs=[vector] * 2,
        out_shape=[half] * 2,
        compiler_params=pltpu.CompilerParams(vmem_limit_bytes=16 * MIB),
        cost_estimate=cost(CUT_FLOPS),
        name="cut",
    )(info, held, *arrived, after)


def extra_kernel(info, temps, kept, fresh, _, near, *refs):
    far, out = refs[:-1], refs[-1]
    half, extras, tokens, wide = near.shape
    peers = 2 * half
    me = lax.axis_index("pos")
    share = mirrored(me, peers) * (wide // HEAD_DIM)
    live = masks(info, info.shape[0] - AHEAD + HOT, extras, tokens, kept.shape[1])
    before = peers.bit_length() - 2
    hot = info[info.shape[0] - 1]
    have = lax.shift_right_logical(me, before) == lax.shift_right_logical(hot, before)
    base = jnp.bitwise_and(me, half)
    sources = [(base + at, near[at]) for at in range(half)]
    sources += [(jnp.bitwise_xor(me, half + at), source[...]) for at, source in enumerate(far)]
    for head in range(wide // HEAD_DIM):
        cols = slice(head * HEAD_DIM, (head + 1) * HEAD_DIM)
        valued = jnp.where(have, kept[head], fresh[head])
        keyed = unit(valued.astype(jnp.float32)).astype(jnp.bfloat16).T
        heat = temps[share + head] * (LOG2E / HEAD_DIM)
        for peer, source in sources:
            query = source[:, :, cols].astype(jnp.float32)
            query = query.reshape(extras * tokens, HEAD_DIM)
            done = softened(query, keyed, valued, heat, live)
            done = done.reshape(1, extras, tokens, HEAD_DIM).astype(jnp.bfloat16)
            out[pl.ds(peer, 1), :, :, cols] = done


def attend_extra(info, temps, kept, fresh, after, near, far, wide):
    half, extras, tokens, held = near.shape
    scalars = pl.BlockSpec(memory_space=pltpu.SMEM)
    rows = pl.BlockSpec(kept.shape, lambda i: (0, 0, 0))
    return pl.pallas_call(
        extra_kernel,
        grid=(1,),
        in_specs=[
            scalars,
            scalars,
            rows,
            rows,
            pl.BlockSpec(memory_space=pl.ANY),
            pl.BlockSpec((half, extras, tokens, wide), lambda i: (0, 0, 0, held // wide - 1)),
        ]
        + [pl.BlockSpec((extras, tokens, wide), lambda i: (0, 0, held // wide - 1))] * half,
        out_specs=pl.BlockSpec((2 * half, extras, tokens, wide), lambda i: (0, 0, 0, 0)),
        out_shape=jax.ShapeDtypeStruct((2 * half, extras, tokens, wide), jnp.bfloat16),
        compiler_params=pltpu.CompilerParams(vmem_limit_bytes=16 * MIB),
        cost_estimate=cost(ATTEND_FLOPS),
        name="attend_extra",
    )(info, temps, kept, fresh, after, near, *far)


def mirrored_number(index, peers):
    bits = peers.bit_length() - 1
    return sum(((index >> bit) & 1) << (bits - 1 - bit) for bit in range(bits))


def mirrored(index, peers):
    result = jnp.int32(0)
    for bit in range(peers.bit_length() - 1):
        result = result * 2 + jnp.bitwise_and(lax.shift_right_logical(index, bit), 1)
    return result


def route(info, peers, slots, extras, rows, blocks, sites):
    me = lax.axis_index("pos")
    ahead = info.shape[0] - AHEAD
    hot_at = info.shape[0] - 1

    def clear(at, carry):
        info[at] = -1
        return carry

    lax.fori_loop(0, info.shape[0], clear, 0)
    for window in range(blocks.shape[0]):
        block = blocks[window]
        count = jnp.int32(0)
        for slot in range(HOT - 1):
            count += (info[block * HOT + slot] >= 0).astype(jnp.int32)
        info[block * HOT + count] = window

        @pl.when(count == HOT - 1)
        def _():
            info[hot_at] = block

    hot = info[hot_at]

    def offset(entry):
        window = info[entry]
        site = sites[jnp.maximum(window, 0)]
        return jnp.where(window >= 0, site - rows * (entry // HOT), rows)

    for slot in range(HOT):
        info[ahead + slot] = offset(me * HOT + slot)
    for extra in range(extras):
        info[ahead + HOT + extra] = offset(hot * HOT + slots + extra)


def deliver(info, queries, targets, sems, slots, extras, peers):
    chans = queries.shape[2]
    hot = info[info.shape[0] - 1]
    copies = []
    for peer, out in targets:
        held = out.shape[2]
        for slot in range(slots):
            window = jnp.maximum(info[peer * HOT + slot], 0)
            copies.append((queries.at[window], out.at[slot, :, pl.ds(0, chans)]))
        for extra in range(extras):
            wide = held - chans
            share = pl.multiple_of(mirrored(peer, peers) * wide, wide)
            window = info[hot * HOT + slots + extra]
            target = out.at[extra, :, pl.ds(chans, wide)]
            copies.append((queries.at[window, :, pl.ds(share, wide)], target))
    copies = [pltpu.make_async_copy(*pair, sems.at[at]) for at, pair in enumerate(copies)]
    for copy in copies:
        copy.start()
    for copy in copies:
        copy.wait()


def near_kernel(extras, rows, blocks, sites, queries, _, info, near, sems, blocks_held, sites_held, pair):
    half, slots, _, _ = near.shape
    loads = [
        pltpu.make_async_copy(blocks, blocks_held, pair.at[0]),
        pltpu.make_async_copy(sites, sites_held, pair.at[1]),
    ]
    for load in loads:
        load.start()
    for load in loads:
        load.wait()
    route(info, 2 * half, slots, extras, rows, blocks_held, sites_held)
    base = jnp.bitwise_and(lax.axis_index("pos"), half)
    targets = [(base + at, near.at[at]) for at in range(half)]
    deliver(info, queries, targets, sems, slots, extras, 2 * half)


def far_kernel(extras, info, queries, _, *refs):
    far, sems = refs[:-1], refs[-1]
    half = len(far)
    me = lax.axis_index("pos")
    targets = [(jnp.bitwise_xor(me, half + at), out) for at, out in enumerate(far)]
    deliver(info, queries, targets, sems, far[0].shape[0], extras, 2 * half)


def pack(blocks, sites, queries, tail, rows, peers, slots):
    windows, tokens, chans = queries.shape
    extras = HOT - slots
    half = peers // 2
    held = chans + (chans // peers if extras else 0)
    scalars = pl.BlockSpec(memory_space=pltpu.SMEM)
    vector = pl.BlockSpec(memory_space=pltpu.VMEM)
    anywhere = pl.BlockSpec(memory_space=pl.ANY)
    hbm = pl.BlockSpec(memory_space=pltpu.HBM)
    message = jax.ShapeDtypeStruct((slots, tokens, held), queries.dtype)
    params = dict(
        compiler_params=pltpu.CompilerParams(vmem_limit_bytes=16 * MIB),
        cost_estimate=cost(PACK_FLOPS),
    )
    sems = pltpu.SemaphoreType.DMA((half * (slots + extras),))
    info, near = pl.pallas_call(
        functools.partial(near_kernel, extras, rows),
        in_specs=[hbm, hbm, hbm, anywhere],
        out_specs=[scalars, vector],
        out_shape=[
            jax.ShapeDtypeStruct((peers * HOT + AHEAD,), jnp.int32),
            jax.ShapeDtypeStruct((half,) + message.shape, queries.dtype),
        ],
        scratch_shapes=[
            sems,
            pltpu.SMEM((windows,), jnp.int32),
            pltpu.SMEM((windows,), jnp.int32),
            pltpu.SemaphoreType.DMA((2,)),
        ],
        name="pack_near",
        **params,
    )(blocks, sites, queries, tail)
    far = pl.pallas_call(
        functools.partial(far_kernel, extras),
        in_specs=[scalars, hbm, anywhere],
        out_specs=[vector] * half,
        out_shape=[message] * half,
        scratch_shapes=[sems],
        name="pack_far",
        **params,
    )(info, queries, near)
    return info, near, far


def unpack_kernel(steps, info, *refs):
    results, out, sems = refs[: len(steps)], refs[-2], refs[-1]
    me = lax.axis_index("pos")
    pieces = []
    for step, result in zip(steps, results):
        if len(result.shape) == 3:
            pieces.append((jnp.bitwise_xor(me, step), result))
        else:
            base = jnp.bitwise_and(me, result.shape[0])
            pieces += [(base + at, result.at[at]) for at in range(result.shape[0])]

    def each(act):
        at = 0
        for peer, result in pieces:
            for slot in range(result.shape[0]):
                window = info[peer * HOT + slot]
                target = out.at[jnp.maximum(window, 0)]
                copy = pltpu.make_async_copy(result.at[slot], target, sems.at[at])
                pl.when(window >= 0)(functools.partial(act, copy))
                at += 1

    each(lambda copy: copy.start())
    each(lambda copy: copy.wait())


def unpack(steps, info, results, so_far, shape, after):
    anywhere = pl.BlockSpec(memory_space=pl.ANY)
    count = len(steps)
    copies = sum(result.size // (shape[1] * shape[2]) for result in results)
    return pl.pallas_call(
        functools.partial(unpack_kernel, steps),
        in_specs=[pl.BlockSpec(memory_space=pltpu.SMEM)]
        + [pl.BlockSpec(memory_space=pltpu.VMEM)] * count
        + [anywhere] * (len(so_far) + 1),
        out_specs=anywhere,
        out_shape=jax.ShapeDtypeStruct(shape, results[0].dtype),
        input_output_aliases={1 + count: 0} if so_far else {},
        scratch_shapes=[pltpu.SemaphoreType.DMA((copies,))],
        compiler_params=pltpu.CompilerParams(vmem_limit_bytes=16 * MIB),
        cost_estimate=cost(CUT_FLOPS),
        name="unpack",
    )(info, *results, *so_far, after)


def unpack_extra_kernel(slots, info, results, _, out, held, sems):
    peers, extras, _, wide = results.shape
    hot = info[info.shape[0] - 1]
    copies = []
    for extra in range(extras):
        for peer in range(peers):
            start = mirrored_number(peer, peers) * wide
            held[extra, :, start : start + wide] = results[peer, extra]
        window = info[hot * HOT + slots + extra]
        copies.append(pltpu.make_async_copy(held.at[extra], out.at[window], sems.at[extra]))
        copies[-1].start()
    for copy in copies:
        copy.wait()


def unpack_extra(info, results, so_far, slots):
    _, extras, tokens, _ = results.shape
    scalars = pl.BlockSpec(memory_space=pltpu.SMEM)
    vector = pl.BlockSpec(memory_space=pltpu.VMEM)
    anywhere = pl.BlockSpec(memory_space=pl.ANY)
    return pl.pallas_call(
        functools.partial(unpack_extra_kernel, slots),
        in_specs=[scalars, vector, anywhere],
        out_specs=anywhere,
        out_shape=jax.ShapeDtypeStruct(so_far.shape, so_far.dtype),
        input_output_aliases={2: 0},
        scratch_shapes=[
            pltpu.VMEM((extras, tokens, so_far.shape[2]), so_far.dtype),
            pltpu.SemaphoreType.DMA((extras,)),
        ],
        compiler_params=pltpu.CompilerParams(vmem_limit_bytes=24 * MIB),
        cost_estimate=cost(1000),
        name="unpack_extra",
    )(info, results, so_far)


def exchanged(value, step):
    peers = lax.axis_size("pos")
    if step == 0:
        return value
    return lax.ppermute(value, "pos", [(i, i ^ step) for i in range(peers)])


def exchanged_near(value):
    peers = lax.axis_size("pos")
    half = peers // 2
    groups = [list(range(half)), list(range(half, peers))]
    return lax.all_to_all(value, "pos", 0, 0, axis_index_groups=groups, tiled=True)


def shards(gate_stream, key_stream, value_stream, filters, temps, queries, blocks, sites):
    rows, chans = gate_stream.shape
    taps = filters.shape[1]
    peers = lax.axis_size("pos")
    me = lax.axis_index("pos").astype(jnp.int32)
    windows = blocks.shape[0]
    heads = chans // HEAD_DIM
    extras = 2 if heads % peers == 0 else 0
    slots = HOT - extras
    wide = chans // peers

    last = slice(rows - taps, rows)
    tail = key_stream[last].astype(jnp.float32) * value_stream[last].astype(jnp.float32)
    tail = tail.astype(jnp.bfloat16)
    earlier = lax.ppermute(tail, "pos", [(i, i + 1) for i in range(peers - 1)])
    info, near, far = pack(blocks, sites, queries, tail, rows, peers, slots)
    half = peers // 2
    far = [exchanged(message, half + at) for at, message in enumerate(far)]
    near = exchanged_near(near)
    hyena_out, valued, keyed = mix(gate_stream, key_stream, value_stream, earlier, filters)

    def attended_far(first, count, after):
        results = attend(info, temps, keyed, valued, after, far[first : first + count])
        moved = [exchanged(result, half + first + at) for at, result in enumerate(results)]
        return moved, results[0]

    bits = peers.bit_length() - 1 if extras else 0
    kept, fresh, after = valued, [], valued
    returned, so_far, done = [], [], 0
    for bit in range(min(bits, 1)):
        sent, kept = cut(bit, info, kept, fresh, after)
        fresh, after = [exchanged(sent, 1 << bit)], sent
    (result,) = attend(info, temps, keyed, valued, after, [near])
    returned_near, after = exchanged_near(result), result
    first = 0
    for place in range(half):
        if first >= half:
            break
        count = 1 if place < 2 else 2
        moved, after = attended_far(first, count, after)
        returned += moved
        first += count
        bit = place + 1
        if bit < bits:
            sent, kept = cut(bit, info, kept, fresh, after)
            fresh, after = [exchanged(sent, 1 << bit)], sent
        if place >= 2:
            early = list(range(half + done, half + done + 2))
            arrivals = returned[done : done + 2]
            so_far = [unpack(early, info, arrivals, so_far, queries.shape, after)]
            after = so_far[0]
            done += 2
    extra_results = []
    if extras:
        result = attend_extra(info, temps, kept, fresh[0], after, near, far, wide)
        extra_results.append(lax.all_to_all(result, "pos", 0, 0, tiled=True))
        after = result
    so_far = [unpack([0], info, [returned_near], so_far, queries.shape, after)]
    late = list(range(half + done, peers))
    so_far = [unpack(late, info, returned[done:], so_far, queries.shape, info)]
    attended = so_far[0]
    for result in extra_results:
        attended = unpack_extra(info, result, attended, slots)
    return (hyena_out, attended)


def solution(mesh):
    placed = (
        P(("groups", "pos"), "mp"),
        P(("groups", "pos"), "mp"),
        P(("groups", "pos"), "mp"),
        P("mp", None),
        P("mp"),
        P("groups", "pos", "mp"),
        P("groups"),
        P("groups"),
    )
    return jax.shard_map(
        shards,
        mesh=mesh,
        in_specs=placed,
        out_specs=(P(("groups", "pos"), "mp"), P("groups", "pos", "mp")),
        check_vma=False,
    )
```

```python
import functools

import jax
import jax.numpy as jnp
import numpy as np
from jax import lax
from jax.experimental import pallas as pl
from jax.experimental.pallas import tpu as pltpu
from jax.sharding import PartitionSpec as P

HEAD_DIM = 128
HOT = 4
EPS = 1e-06
LOG2E = 1.4426950408889634
MIB = 1 << 20
AHEAD = 16
PACK_VMEM = 60
ATTEND_FLOPS = 20 << 30
MIX_FLOPS = 100 << 30
PACK_FLOPS = 20 << 30


def cost(flops):
    return pl.CostEstimate(flops=flops, bytes_accessed=1000, transcendentals=0)


def halves(array):
    high = array.astype(jnp.bfloat16)
    low = (array - high.astype(jnp.float32)).astype(jnp.bfloat16)
    return high, low


def transforms(taps):
    size = 2 * taps
    odd = 2 * np.arange(taps) + 1
    angle = np.pi / size * ((odd[:, None] * np.arange(size)[None, :]) % (2 * size))
    forward = np.concatenate([np.cos(angle), -np.sin(angle)], 0)
    inverse = forward.T[taps:] * (2.0 / size)
    out = []
    for matrix in (forward, inverse):
        high = matrix.astype(jnp.bfloat16)
        low = (matrix - high.astype(np.float64)).astype(jnp.bfloat16)
        out.append(np.concatenate([high, low], 0))
    return out


def unit(block):
    return block * lax.rsqrt(jnp.mean(block * block, axis=-1, keepdims=True) + EPS)


def mix_kernel(gate, key, value, earlier, filters, forward, inverse, _, out, rows_of, keys_of):
    rows, wide = gate.shape
    taps = filters.shape[1]
    size = 2 * taps
    f32 = jnp.float32
    fwd = forward[...]
    inv = inverse[...]
    high, low = halves(filters[...])
    across = (((1,), (1,)), ((), ()))
    both = lax.dot_general(fwd[:, :taps], high, across, preferred_element_type=f32)
    spectrum = both[:size] + both[size:]
    spectrum += lax.dot_general(fwd[:size, :taps], low, across, preferred_element_type=f32)
    hr, hi = spectrum[:taps], spectrum[taps:]
    before = earlier[...]
    for start in range(0, rows, taps):
        part = slice(start, start + taps)
        now = (key[part, :].astype(f32) * value[part, :].astype(f32)).astype(jnp.bfloat16)
        both = jnp.dot(fwd, jnp.concatenate([before, now], 0), preferred_element_type=f32)
        seen = both[:size] + both[size:]
        xr, xi = seen[:taps], seen[taps:]
        product = jnp.concatenate([xr * hr - xi * hi, xr * hi + xi * hr], 0)
        high, low = halves(product)
        both = jnp.dot(inv, high, preferred_element_type=f32)
        mixed = both[:taps] + both[taps:]
        mixed += jnp.dot(inv[:taps], low, preferred_element_type=f32)
        result = (gate[part, :].astype(f32) * mixed).astype(jnp.bfloat16)
        out[part, :] = result
        for head in range(wide // HEAD_DIM):
            piece = result[:, head * HEAD_DIM : (head + 1) * HEAD_DIM]
            rows_of[head, part, :] = piece
            keys_of[head, :, part] = unit(piece.astype(f32)).astype(jnp.bfloat16).T
        before = now


def mix(gate, key, value, earlier, filters, after):
    rows, chans = gate.shape
    taps = filters.shape[1]
    heads = chans // HEAD_DIM
    wide = 2 * HEAD_DIM
    each = wide // HEAD_DIM
    forward, inverse = (jnp.asarray(matrix) for matrix in transforms(taps))
    stream = pl.BlockSpec((rows, wide), lambda i: (0, i))
    by_head = pl.BlockSpec((each, rows, HEAD_DIM), lambda i: (i, 0, 0))
    whole = lambda array: pl.BlockSpec(array.shape, lambda i: (0, 0))
    turned = pl.BlockSpec((each, HEAD_DIM, rows), lambda i: (i, 0, 0))
    per_head = jax.ShapeDtypeStruct((heads, rows, HEAD_DIM), jnp.bfloat16)
    per_head_turned = jax.ShapeDtypeStruct((heads, HEAD_DIM, rows), jnp.bfloat16)
    return pl.pallas_call(
        mix_kernel,
        grid=(chans // wide,),
        in_specs=[
            stream,
            stream,
            stream,
            pl.BlockSpec((taps, wide), lambda i: (0, i)),
            pl.BlockSpec((wide, taps), lambda i: (i, 0)),
            whole(forward),
            whole(inverse),
            pl.BlockSpec(memory_space=pl.ANY),
        ],
        out_specs=[stream, by_head, turned],
        out_shape=[jax.ShapeDtypeStruct((rows, chans), jnp.bfloat16), per_head, per_head_turned],
        compiler_params=pltpu.CompilerParams(vmem_limit_bytes=48 * MIB),
        cost_estimate=cost(MIX_FLOPS),
        name="mix",
    )(gate, key, value, earlier, filters, forward, inverse, after)


def softened(query, keys, rows, heat, live):
    f32 = jnp.float32
    query = unit(query).astype(jnp.bfloat16)
    scores = jnp.dot(query, keys, preferred_element_type=f32)
    weights = jnp.where(live, jnp.exp2(scores * heat), 0.0)
    total = jnp.sum(weights, axis=-1, keepdims=True)
    return jnp.dot(weights.astype(jnp.bfloat16), rows, preferred_element_type=f32) / total


def masks(offsets, first, slots, tokens, positions):
    place = lax.broadcasted_iota(jnp.int32, (tokens, positions), 1)
    return jnp.concatenate([place < offsets[first + slot] for slot in range(slots)], 0)


def attend_heads(info, temps, keys, rows, places, first, last):
    positions = keys.shape[2]
    slots, tokens = places[0][:2]
    each = slots * tokens
    live = masks(info, info.shape[0] - AHEAD, slots, tokens, positions)
    live = jnp.concatenate([live] * len(places), 0)

    def one(head, carry):
        query = [load(head).astype(jnp.float32).reshape(each, HEAD_DIM) for _, _, load, _ in places]
        heat = temps[head] * (LOG2E / HEAD_DIM)
        done = softened(jnp.concatenate(query, 0), keys[head], rows[head], heat, live)
        for place, (_, _, _, store) in enumerate(places):
            part = done[place * each : (place + 1) * each].reshape(slots, tokens, HEAD_DIM)
            store(head, part.astype(jnp.bfloat16))
        return carry

    lax.fori_loop(first, last, one, 0, unroll=2 if (last - first) % 2 == 0 else 1)


def columns(head):
    return pl.ds(pl.multiple_of(head * HEAD_DIM, HEAD_DIM), HEAD_DIM)


def loader(ref, shift, *at):
    return lambda head: ref[at + (slice(None), slice(None), columns(head - shift))]


def storer(ref, shift, *at):
    def store(head, block):
        ref[at + (slice(None), slice(None), columns(head - shift))] = block

    return store


def near_kernel(info, temps, keys, rows, _, near, out):
    half, slots, tokens, _ = near.shape
    places = [(slots, tokens, loader(near, 0, at), storer(out, 0, at)) for at in range(half)]
    attend_heads(info, temps, keys, rows, places, 0, keys.shape[0])


def first_kernel(tail, info, temps, keys, rows, _, queries, rest, out, kept):
    slots, tokens, _ = queries.shape
    heads = keys.shape[0]
    split = heads - 2 * tail
    for_out = [(slots, tokens, loader(queries, 0), storer(out, 0))]
    attend_heads(info, temps, keys, rows, for_out, 0, split)
    for_kept = [(slots, tokens, loader(queries, 0), storer(kept, split))]
    attend_heads(info, temps, keys, rows, for_kept, split, heads - tail)
    part = slice(split * HEAD_DIM, (split + tail) * HEAD_DIM)
    home = on_hot_half(info, out_peers(heads, tail))

    @pl.when(home)
    def _():
        out[:, :, part] = kept[...]

    @pl.when(jnp.logical_not(home))
    def _():
        out[:, :, part] = rest[...]


def second_kernel(tail, step, info, temps, keys, rows, extra, _, queries, later, kept, out, held):
    slots, tokens, _ = queries.shape
    heads = keys.shape[0]
    split = heads - 2 * tail
    home = on_hot_half(info, out_peers(heads, tail))

    @pl.when(home)
    def _():
        held[...] = later[:, :, split * HEAD_DIM :]

    @pl.when(jnp.logical_not(home))
    def _():
        held[...] = queries[:, :, (split + tail) * HEAD_DIM :]

    places = [(slots, tokens, loader(held, heads - tail), storer(out, heads - tail))]
    attend_heads(info, temps, keys, rows, places, heads - tail, heads)
    part = slice(tail * HEAD_DIM, 2 * tail * HEAD_DIM)

    @pl.when(home)
    def _():
        out[:, :, part] = extra[jnp.bitwise_xor(lax.axis_index("pos"), step)]

    @pl.when(jnp.logical_not(home))
    def _():
        out[:, :, part] = kept[...]


def out_peers(heads, tail):
    return 2 * (heads // tail)


def on_hot_half(info, peers):
    half = peers // 2
    return (lax.axis_index("pos") >= half) == (info[info.shape[0] - 1] >= half)


def attend(kernel, name, widths, info, temps, keys, rows, refs, unread, arrays, scratch=()):
    scalars = pl.BlockSpec(memory_space=pltpu.SMEM)
    vector = pl.BlockSpec(memory_space=pltpu.VMEM)
    anywhere = pl.BlockSpec(memory_space=pl.ANY)
    leading = arrays[0].shape[:-1]
    return pl.pallas_call(
        kernel,
        in_specs=[scalars, scalars, vector, vector]
        + [vector] * len(refs)
        + [anywhere]
        + [vector] * len(arrays),
        out_specs=[vector] * len(widths),
        out_shape=[
            jax.ShapeDtypeStruct(leading + (width * HEAD_DIM,), jnp.bfloat16) for width in widths
        ],
        scratch_shapes=list(scratch),
        compiler_params=pltpu.CompilerParams(vmem_limit_bytes=16 * MIB),
        cost_estimate=cost(ATTEND_FLOPS),
        name=name,
    )(info, temps, keys, rows, *refs, unread, *arrays)


def finish_kernel(extra, near, out):
    half, _, _, chans = near.shape
    base = jnp.bitwise_and(lax.axis_index("pos"), half)
    out[:, :, :, :chans] = near[...]
    for at in range(half):
        out[at, :, :, chans:] = extra[base + at]


def finish(extra, near):
    vector = pl.BlockSpec(memory_space=pltpu.VMEM)
    held = near.shape[3] + extra.shape[3]
    return pl.pallas_call(
        finish_kernel,
        in_specs=[vector] * 2,
        out_specs=vector,
        out_shape=jax.ShapeDtypeStruct(near.shape[:3] + (held,), jnp.bfloat16),
        compiler_params=pltpu.CompilerParams(vmem_limit_bytes=24 * MIB),
        cost_estimate=cost(1000),
        name="finish",
    )(extra, near)


def extra_kernel(info, temps, rows, _, near, *refs):
    far, out = refs[:-1], refs[-1]
    half, extras, tokens, wide = near.shape
    me = lax.axis_index("pos")
    hot = jnp.bitwise_and(info[info.shape[0] - 1], half - 1)
    each = wide // HEAD_DIM
    first = jnp.bitwise_and(me, half - 1) * each
    live = masks(info, info.shape[0] - AHEAD + HOT, extras, tokens, rows.shape[2])
    live = jnp.concatenate([live] * half, 0)
    base = jnp.bitwise_and(me, half)
    for head in range(each):
        cols = slice(head * HEAD_DIM, (head + 1) * HEAD_DIM)
        valued = rows[hot, head]
        keyed = unit(valued.astype(jnp.float32)).astype(jnp.bfloat16).T
        heat = temps[first + head] * (LOG2E / HEAD_DIM)
        for side in range(2):
            query = [source[:, :, cols] for source in far] if side else [near[:, :, :, cols]]
            query = [part.astype(jnp.float32).reshape(-1, HEAD_DIM) for part in query]
            done = softened(jnp.concatenate(query, 0), keyed, valued, heat, live)
            done = done.reshape(half, extras, tokens, HEAD_DIM).astype(jnp.bfloat16)
            for at in range(half):
                peer = jnp.bitwise_xor(me, half + at) if side else base + at
                out[pl.ds(peer, 1), :, :, cols] = done[at : at + 1]


def attend_extra(info, temps, rows, after, near, far, wide):
    half, extras, tokens, held = near.shape
    scalars = pl.BlockSpec(memory_space=pltpu.SMEM)
    return pl.pallas_call(
        extra_kernel,
        grid=(1,),
        in_specs=[
            scalars,
            scalars,
            pl.BlockSpec(rows.shape, lambda i: (0, 0, 0, 0)),
            pl.BlockSpec(memory_space=pl.ANY),
            pl.BlockSpec((half, extras, tokens, wide), lambda i: (0, 0, 0, held // wide - 1)),
        ]
        + [pl.BlockSpec((extras, tokens, wide), lambda i: (0, 0, held // wide - 2))] * half,
        out_specs=pl.BlockSpec((2 * half, extras, tokens, wide), lambda i: (0, 0, 0, 0)),
        out_shape=jax.ShapeDtypeStruct((2 * half, extras, tokens, wide), jnp.bfloat16),
        compiler_params=pltpu.CompilerParams(vmem_limit_bytes=16 * MIB),
        cost_estimate=cost(ATTEND_FLOPS),
        name="attend_extra",
    )(info, temps, rows, after, near, *far)


def route(info, peers, slots, extras, rows, blocks, sites):
    me = lax.axis_index("pos")
    ahead = info.shape[0] - AHEAD
    hot_at = info.shape[0] - 1

    def clear(at, carry):
        info[at] = -1
        return carry

    lax.fori_loop(0, info.shape[0], clear, 0)
    for window in range(blocks.shape[0]):
        block = blocks[window]
        count = jnp.int32(0)
        for slot in range(HOT - 1):
            count += (info[block * HOT + slot] >= 0).astype(jnp.int32)
        info[block * HOT + count] = window

        @pl.when(count == HOT - 1)
        def _():
            info[hot_at] = block

    hot = info[hot_at]

    def offset(entry):
        window = info[entry]
        site = sites[jnp.maximum(window, 0)]
        return jnp.where(window >= 0, site - rows * (entry // HOT), rows)

    for slot in range(HOT):
        info[ahead + slot] = offset(me * HOT + slot)
    for extra in range(extras):
        info[ahead + HOT + extra] = offset(hot * HOT + slots + extra)


def copied(copies, sems):
    copies = [pltpu.make_async_copy(*pair, sems.at[at]) for at, pair in enumerate(copies)]
    for copy in copies:
        copy.start()
    for copy in copies:
        copy.wait()


def message(info, queries, peer, out, wide, extras, start, count, with_extras):
    slots, _, held = out.shape
    hot = info[info.shape[0] - 1]
    copies = []
    for slot in range(slots):
        window = jnp.maximum(info[peer * HOT + slot], 0)
        source = queries.at[window, :, pl.ds(start, count)]
        copies.append((source, out.at[slot, :, pl.ds(0, count)]))
    half = queries.shape[2] // wide
    share = pl.multiple_of(jnp.bitwise_and(peer, half - 1) * wide, wide)
    for extra in range(extras if held > count else 0):
        window = info[hot * HOT + slots + extra]
        column = share
        if with_extras is not None:
            window = jnp.where(with_extras, window, jnp.maximum(info[peer * HOT + extra], 0))
            column = pl.multiple_of(jnp.where(with_extras, share, start + count), wide)
        source = queries.at[window, :, pl.ds(column, wide)]
        copies.append((source, out.at[extra, :, pl.ds(count, wide)]))
    return copies


def far_copies(info, queries, steps, far, rest, wide, extras):
    half = queries.shape[2] // wide
    me = lax.axis_index("pos")
    away = jnp.logical_not(on_hot_half(info, 2 * half))
    chans = queries.shape[2]
    copies = []
    for step, out, other in zip(steps, far, rest):
        peer = jnp.bitwise_xor(me, step)
        copies += message(info, queries, peer, out, wide, extras, 0, chans - wide, away)
        copies += message(info, queries, peer, other, wide, extras, chans - wide, wide, None)
    return copies


def pack_kernel(extras, rows, wide, blocks, sites, queries, _, info, near, *refs):
    half, slots, _, _ = near.shape
    outs, (sems, blocks_held, sites_held, pair) = refs[:-4], refs[-4:]
    count = len(outs) // 2
    copied([(blocks, blocks_held), (sites, sites_held)], pair)
    route(info, 2 * half, slots, extras, rows, blocks_held, sites_held)
    base = jnp.bitwise_and(lax.axis_index("pos"), half)
    chans = queries.shape[2]
    steps = range(half, half + count)
    copies = far_copies(info, queries, steps, outs[:count], outs[count:], wide, extras)
    for at in range(half):
        copies += message(info, queries, base + at, near.at[at], wide, extras, 0, chans, None)
    copied(copies, sems)


def pack_later_kernel(extras, wide, steps, info, queries, _, *refs):
    outs, sems = refs[:-1], refs[-1]
    count = len(outs) // 2
    copied(far_copies(info, queries, steps, outs[:count], outs[count:], wide, extras), sems)


def far_shapes(queries, slots, wide, count):
    _, tokens, chans = queries.shape
    return [jax.ShapeDtypeStruct((slots, tokens, chans), queries.dtype)] * count + [
        jax.ShapeDtypeStruct((slots, tokens, wide), queries.dtype)
    ] * count


def pack(blocks, sites, queries, tail, rows, half, slots, extras, wide, count):
    windows, tokens, chans = queries.shape
    scalars = pl.BlockSpec(memory_space=pltpu.SMEM)
    vector = pl.BlockSpec(memory_space=pltpu.VMEM)
    anywhere = pl.BlockSpec(memory_space=pl.ANY)
    info, near, *far = pl.pallas_call(
        functools.partial(pack_kernel, extras, rows, wide),
        in_specs=[anywhere] * 4,
        out_specs=[scalars] + [vector] * (1 + 2 * count),
        out_shape=[
            jax.ShapeDtypeStruct((2 * half * HOT + AHEAD,), jnp.int32),
            jax.ShapeDtypeStruct((half, slots, tokens, chans + wide), queries.dtype),
        ]
        + far_shapes(queries, slots, wide, count),
        scratch_shapes=[
            pltpu.SemaphoreType.DMA(((half + count) * (slots + extras) + count * slots,)),
            pltpu.SMEM((windows,), jnp.int32),
            pltpu.SMEM((windows,), jnp.int32),
            pltpu.SemaphoreType.DMA((2,)),
        ],
        compiler_params=pltpu.CompilerParams(vmem_limit_bytes=PACK_VMEM * MIB),
        cost_estimate=cost(PACK_FLOPS),
        name="pack",
    )(blocks, sites, queries, tail)
    return info, near, far[:count], far[count:]


def pack_later(info, queries, after, steps, slots, extras, wide):
    count = len(steps)
    vector = pl.BlockSpec(memory_space=pltpu.VMEM)
    anywhere = pl.BlockSpec(memory_space=pl.ANY)
    far = pl.pallas_call(
        functools.partial(pack_later_kernel, extras, wide, steps),
        in_specs=[pl.BlockSpec(memory_space=pltpu.SMEM), anywhere, anywhere],
        out_specs=[vector] * (2 * count),
        out_shape=far_shapes(queries, slots, wide, count),
        scratch_shapes=[pltpu.SemaphoreType.DMA((count * (2 * slots + extras),))],
        compiler_params=pltpu.CompilerParams(vmem_limit_bytes=PACK_VMEM * MIB),
        cost_estimate=cost(1000),
        name="pack_later",
    )(info, queries, after)
    return far[:count], far[count:]


def placed(info, out, sems, pieces):
    def each(act):
        at = 0
        for peer, result, start, count, column, whether in pieces:
            for slot in range(result.shape[0]):
                window = info[peer * HOT + slot]
                source = result.at[slot, :, pl.ds(start, count)]
                target = out.at[jnp.maximum(window, 0), :, pl.ds(column, count)]
                copy = pltpu.make_async_copy(source, target, sems.at[at])
                pl.when(jnp.logical_and(window >= 0, whether))(functools.partial(act, copy))
                at += 1

    each(lambda copy: copy.start())
    return lambda: each(lambda copy: copy.wait())


def unpack_early_kernel(wide, info, *refs):
    results, out, sems = refs[:-3], refs[-2], refs[-1]
    half = len(results)
    me = lax.axis_index("pos")
    home = on_hot_half(info, 2 * half)
    split = out.shape[2] - 2 * wide
    pieces = []
    for at, result in enumerate(results):
        peer = jnp.bitwise_xor(me, half + at)
        pieces.append((peer, result, 0, split, 0, True))
        pieces.append((peer, result, split, wide, split, jnp.logical_not(home)))
    placed(info, out, sems, pieces)()


def unpack_early(info, results, after, shape, wide):
    anywhere = pl.BlockSpec(memory_space=pl.ANY)
    count = len(results)
    return pl.pallas_call(
        functools.partial(unpack_early_kernel, wide),
        in_specs=[pl.BlockSpec(memory_space=pltpu.SMEM)]
        + [pl.BlockSpec(memory_space=pltpu.VMEM)] * count
        + [anywhere],
        out_specs=anywhere,
        out_shape=jax.ShapeDtypeStruct(shape, results[0].dtype),
        scratch_shapes=[pltpu.SemaphoreType.DMA((2 * count * results[0].shape[0],))],
        compiler_params=pltpu.CompilerParams(vmem_limit_bytes=16 * MIB),
        cost_estimate=cost(1000),
        name="unpack_early",
    )(info, *results, after)


def unpack_kernel(wide, info, near, *refs):
    half, slots, _, _ = near.shape
    far, (_, out, own, far_sems, near_sems, own_sems) = refs[:half], refs[half:]
    chans = out.shape[2]
    split = chans - 2 * wide
    me = lax.axis_index("pos")
    base = jnp.bitwise_and(me, half)
    hot = info[info.shape[0] - 1]
    home = on_hot_half(info, 2 * half)
    pieces = []
    for at, result in enumerate(far):
        peer = jnp.bitwise_xor(me, half + at)
        pieces.append((peer, result, 0, wide, split + wide, True))
        pieces.append((peer, result, wide, wide, split, home))
    far_wait = placed(info, out, far_sems, pieces)
    pieces = [(base + at, near.at[at], 0, chans, 0, True) for at in range(half)]
    near_wait = placed(info, out, near_sems, pieces)
    copies = []
    for extra in range(own.shape[0]):

        @pl.when(home)
        def _():
            for at in range(half):
                own[extra, :, at * wide : (at + 1) * wide] = near[at, extra, :, chans:]

        @pl.when(jnp.logical_not(home))
        def _():
            for at, result in enumerate(far):
                share = jnp.bitwise_and(jnp.bitwise_xor(me, at), half - 1)
                cols = pl.ds(pl.multiple_of(share * wide, wide), wide)
                own[extra, :, cols] = result[extra, :, wide:]

        window = info[hot * HOT + slots + extra]
        copies.append(pltpu.make_async_copy(own.at[extra], out.at[window], own_sems.at[extra]))
        copies[-1].start()
    far_wait()
    near_wait()
    for copy in copies:
        copy.wait()


def unpack(info, near, far, so_far, extras, wide):
    half, slots, tokens, _ = near.shape
    anywhere = pl.BlockSpec(memory_space=pl.ANY)
    return pl.pallas_call(
        functools.partial(unpack_kernel, wide),
        in_specs=[pl.BlockSpec(memory_space=pltpu.SMEM)]
        + [pl.BlockSpec(memory_space=pltpu.VMEM)] * (1 + half)
        + [anywhere],
        out_specs=anywhere,
        out_shape=jax.ShapeDtypeStruct(so_far.shape, so_far.dtype),
        input_output_aliases={2 + half: 0},
        scratch_shapes=[
            pltpu.VMEM((extras, tokens, so_far.shape[2]), so_far.dtype),
            pltpu.SemaphoreType.DMA((2 * half * slots,)),
            pltpu.SemaphoreType.DMA((half * slots,)),
            pltpu.SemaphoreType.DMA((extras,)),
        ],
        compiler_params=pltpu.CompilerParams(vmem_limit_bytes=24 * MIB),
        cost_estimate=cost(1000),
        name="unpack",
    )(info, near, *far, so_far)


def wait_kernel(*_):
    pass


def once(value, after):
    anywhere = pl.BlockSpec(memory_space=pl.ANY)
    return pl.pallas_call(
        wait_kernel,
        in_specs=[anywhere] * 2,
        out_specs=anywhere,
        out_shape=jax.ShapeDtypeStruct(value.shape, value.dtype),
        input_output_aliases={0: 0},
        cost_estimate=cost(1000),
        name="once",
    )(value, after)


def exchanged(value, step):
    peers = lax.axis_size("pos")
    if step == 0:
        return value
    return lax.ppermute(value, "pos", [(i, i ^ step) for i in range(peers)])


def exchanged_near(value):
    peers = lax.axis_size("pos")
    half = peers // 2
    groups = [list(range(half)), list(range(half, peers))]
    return lax.all_to_all(value, "pos", 0, 0, axis_index_groups=groups, tiled=True)


def shards(gate_stream, key_stream, value_stream, filters, temps, queries, blocks, sites):
    rows, chans = gate_stream.shape
    taps = filters.shape[1]
    peers = lax.axis_size("pos")
    me = lax.axis_index("pos").astype(jnp.int32)
    windows = blocks.shape[0]
    heads = chans // HEAD_DIM
    extras = 2
    slots = HOT - extras
    half = peers // 2

    last = slice(rows - taps, rows)
    tail = key_stream[last].astype(jnp.float32) * value_stream[last].astype(jnp.float32)
    tail = tail.astype(jnp.bfloat16)
    earlier = lax.ppermute(tail, "pos", [(i, i + 1) for i in range(peers - 1)])
    wide = chans // half
    share = heads // half
    ahead = half // 2
    info, near, far, rest = pack(
        blocks, sites, queries, tail, rows, half, slots, extras, wide, ahead
    )
    far = [exchanged(sent, half + at) for at, sent in enumerate(far)]
    near = exchanged_near(near)
    hyena_out, valued, keyed = mix(
        gate_stream, key_stream, value_stream, earlier, filters, info
    )
    valued = once(valued, near)
    hot_rows = exchanged_near(valued).reshape((half, share) + valued.shape[1:])
    steps = range(half + ahead, peers)
    far_later, rest_later = pack_later(info, queries, valued, steps, slots, extras, wide)
    far += [exchanged(sent, step) for step, sent in zip(steps, far_later)]
    rest += rest_later

    own = (info, temps, keyed, valued)
    (near_results,) = attend(near_kernel, "attend_near", [heads], *own, [], valued, [near])
    sent, kept, after = [], [], near_results
    for at in range(half):
        kernel = functools.partial(first_kernel, share)
        result, back = attend(
            kernel, "attend_first", [heads - share, share], *own, [], after, [far[at], rest[at]]
        )
        sent.append(exchanged(result, half + at))
        kept.append(back)
        after = result
    extra = attend_extra(info, temps, hot_rows, after, near, far, wide)
    near_out = exchanged_near(finish(extra, near_results))
    late, after = [], extra
    for at in range(half):
        kernel = functools.partial(second_kernel, share, half + at)
        arrays = [far[at], sent[at], kept[at]]
        scratch = [pltpu.VMEM(kept[at].shape, jnp.bfloat16)]
        (result,) = attend(
            kernel, "attend_second", [2 * share], *own, [extra], after, arrays, scratch
        )
        late.append(exchanged(result, half + at))
        after = result
    so_far = unpack_early(info, sent, after, queries.shape, wide)
    return (hyena_out, unpack(info, near_out, late, so_far, extras, wide))


def solution(mesh):
    placed = (
        P(("groups", "pos"), "mp"),
        P(("groups", "pos"), "mp"),
        P(("groups", "pos"), "mp"),
        P("mp", None),
        P("mp"),
        P("groups", "pos", "mp"),
        P("groups"),
        P("groups"),
    )
    return jax.shard_map(
        shards,
        mesh=mesh,
        in_specs=placed,
        out_specs=(P(("groups", "pos"), "mp"), P("groups", "pos", "mp")),
        check_vma=False,
    )
```

```python
import functools

import jax
import jax.numpy as jnp
import numpy as np
from jax import lax
from jax.experimental import pallas as pl
from jax.experimental.pallas import tpu as pltpu
from jax.sharding import PartitionSpec as P

HEAD_DIM = 128
HOT = 4
EPS = 1e-06
LOG2E = 1.4426950408889634
MIB = 1 << 20
AHEAD = 16
UNPACK_FLOPS = 20 << 30
PACK_VMEM = 60
ATTEND_FLOPS = 20 << 30
MIX_FLOPS = 100 << 30
PACK_FLOPS = 20 << 30


def cost(flops):
    return pl.CostEstimate(flops=flops, bytes_accessed=1000, transcendentals=0)


def halves(array):
    high = array.astype(jnp.bfloat16)
    low = (array - high.astype(jnp.float32)).astype(jnp.bfloat16)
    return high, low


def transforms(taps):
    size = 2 * taps
    odd = 2 * np.arange(taps) + 1
    angle = np.pi / size * ((odd[:, None] * np.arange(size)[None, :]) % (2 * size))
    forward = np.concatenate([np.cos(angle), -np.sin(angle)], 0)
    inverse = forward.T[taps:] * (2.0 / size)
    out = []
    for matrix in (forward, inverse):
        high = matrix.astype(jnp.bfloat16)
        low = (matrix - high.astype(np.float64)).astype(jnp.bfloat16)
        out.append(np.concatenate([high, low], 0))
    return out


def unit(block):
    return block * lax.rsqrt(jnp.mean(block * block, axis=-1, keepdims=True) + EPS)


def mix_rows(starts, before, gate, key, value, filters, forward, inverse, out, rows_of, keys_of):
    _, wide = gate.shape
    taps = filters.shape[1]
    size = 2 * taps
    f32 = jnp.float32
    fwd = forward[...]
    inv = inverse[...]
    high, low = halves(filters[...])
    across = (((1,), (1,)), ((), ()))
    both = lax.dot_general(fwd[:, :taps], high, across, preferred_element_type=f32)
    spectrum = both[:size] + both[size:]
    spectrum += lax.dot_general(fwd[:size, :taps], low, across, preferred_element_type=f32)
    hr, hi = spectrum[:taps], spectrum[taps:]
    for start in starts:
        part = slice(start, start + taps)
        now = products(key, value, part)
        both = jnp.dot(fwd, jnp.concatenate([before, now], 0), preferred_element_type=f32)
        seen = both[:size] + both[size:]
        xr, xi = seen[:taps], seen[taps:]
        product = jnp.concatenate([xr * hr - xi * hi, xr * hi + xi * hr], 0)
        high, low = halves(product)
        both = jnp.dot(inv, high, preferred_element_type=f32)
        mixed = both[:taps] + both[taps:]
        mixed += jnp.dot(inv[:taps], low, preferred_element_type=f32)
        result = (gate[part, :].astype(f32) * mixed).astype(jnp.bfloat16)
        out[part, :] = result
        for head in range(wide // HEAD_DIM):
            piece = result[:, head * HEAD_DIM : (head + 1) * HEAD_DIM]
            rows_of[head, part, :] = piece
            keys_of[head, :, part] = unit(piece.astype(f32)).astype(jnp.bfloat16).T
        before = now


def products(key, value, part):
    return (key[part, :].astype(jnp.float32) * value[part, :].astype(jnp.float32)).astype(jnp.bfloat16)


def mix_later_kernel(gate, key, value, filters, forward, inverse, _, *outs):
    taps = filters.shape[1]
    before = products(key, value, slice(0, taps))
    starts = range(taps, gate.shape[0], taps)
    mix_rows(starts, before, gate, key, value, filters, forward, inverse, *outs)


def mix_first_kernel(gate, key, value, filters, forward, inverse, earlier, *refs):
    mix_rows([0], earlier[...], gate, key, value, filters, forward, inverse, *refs[-3:])


def mix(gate, key, value, earlier, filters, after):
    rows, chans = gate.shape
    taps = filters.shape[1]
    heads = chans // HEAD_DIM
    wide = 8 * HEAD_DIM
    forward, inverse = (jnp.asarray(matrix) for matrix in transforms(taps))
    anywhere = pl.BlockSpec(memory_space=pl.ANY)
    whole = lambda array: pl.BlockSpec(array.shape, lambda i: (0, 0))
    first = pl.BlockSpec((taps, wide), lambda i: (0, i))

    def specs(high):
        stream = pl.BlockSpec((high, wide), lambda i: (0, i))
        by_head = pl.BlockSpec((wide // HEAD_DIM, high, HEAD_DIM), lambda i: (i, 0, 0))
        turned = pl.BlockSpec((wide // HEAD_DIM, HEAD_DIM, high), lambda i: (i, 0, 0))
        weights = pl.BlockSpec((wide, taps), lambda i: (i, 0))
        return [stream] * 3 + [weights, whole(forward), whole(inverse)], [stream, by_head, turned]

    params = dict(
        grid=(chans // wide,),
        out_shape=[
            jax.ShapeDtypeStruct((rows, chans), jnp.bfloat16),
            jax.ShapeDtypeStruct((heads, rows, HEAD_DIM), jnp.bfloat16),
            jax.ShapeDtypeStruct((heads, HEAD_DIM, rows), jnp.bfloat16),
        ],
        compiler_params=pltpu.CompilerParams(vmem_limit_bytes=48 * MIB),
        cost_estimate=cost(MIX_FLOPS),
    )
    arrays = (gate, key, value, filters, forward, inverse)
    ins, outs = specs(rows)
    mixed = pl.pallas_call(
        mix_later_kernel, in_specs=ins + [anywhere], out_specs=outs, name="mix_later", **params
    )(*arrays, after)
    ins, outs = specs(taps)
    return pl.pallas_call(
        mix_first_kernel,
        in_specs=ins + [first] + [anywhere] * 3,
        out_specs=outs,
        input_output_aliases={7: 0, 8: 1, 9: 2},
        name="mix_first",
        **params,
    )(*arrays, earlier, *mixed)


def softened(queries, keys, rows, heats, live):
    f32 = jnp.float32
    queries = [unit(query).astype(jnp.bfloat16) for query in queries]
    scores = [jnp.dot(*pair, preferred_element_type=f32) for pair in zip(queries, keys)]
    weights = [jnp.where(live, jnp.exp2(s * heat), 0.0) for s, heat in zip(scores, heats)]
    totals = [jnp.sum(weight, axis=-1, keepdims=True) for weight in weights]
    sums = [
        jnp.dot(weight.astype(jnp.bfloat16), rows_of, preferred_element_type=f32)
        for weight, rows_of in zip(weights, rows)
    ]
    return [part / total for part, total in zip(sums, totals)]


def together(count, high):
    most = 8 if high <= 128 else 4
    return max(size for size in range(1, most + 1) if count % size == 0)


def masks(offsets, first, slots, tokens, positions):
    place = lax.broadcasted_iota(jnp.int32, (tokens, positions), 1)
    return jnp.concatenate([place < offsets[first + slot] for slot in range(slots)], 0)


def attend_heads(info, temps, keys, rows, places, first, last):
    positions = keys.shape[2]
    slots, tokens = places[0][:2]
    each = slots * tokens
    live = masks(info, info.shape[0] - AHEAD, slots, tokens, positions)
    live = jnp.concatenate([live] * len(places), 0)

    batch = together(last - first, each * len(places))

    def some(step, carry):
        heads = [first + step * batch + at for at in range(batch)]
        queries = []
        for head in heads:
            parts = [load(head).astype(jnp.float32) for _, _, load, _ in places]
            queries.append(jnp.concatenate([part.reshape(each, HEAD_DIM) for part in parts], 0))
        heats = [temps[head] * (LOG2E / HEAD_DIM) for head in heads]
        done = softened(queries, [keys[h] for h in heads], [rows[h] for h in heads], heats, live)
        for head, block in zip(heads, done):
            for place, (_, _, _, store) in enumerate(places):
                part = block[place * each : (place + 1) * each].reshape(slots, tokens, HEAD_DIM)
                store(head, part.astype(jnp.bfloat16))
        return carry

    lax.fori_loop(0, (last - first) // batch, some, 0)


def columns(head):
    return pl.ds(pl.multiple_of(head * HEAD_DIM, HEAD_DIM), HEAD_DIM)


def loader(ref, shift, *at):
    return lambda head: ref[at + (slice(None), slice(None), columns(head - shift))]


def storer(ref, shift, *at):
    def store(head, block):
        ref[at + (slice(None), slice(None), columns(head - shift))] = block

    return store


def near_kernel(info, temps, keys, rows, _, near, out):
    half, slots, tokens, _ = near.shape
    places = [(slots, tokens, loader(near, 0, at), storer(out, 0, at)) for at in range(half)]
    attend_heads(info, temps, keys, rows, places, 0, keys.shape[0])


def first_kernel(tail, info, temps, keys, rows, _, queries, rest, out, kept):
    slots, tokens, _ = queries.shape
    heads = keys.shape[0]
    split = heads - 2 * tail
    places = [(slots, tokens, loader(queries, 0), storer(out, 0))]
    attend_heads(info, temps, keys, rows, places, 0, heads - tail)
    part = slice(split * HEAD_DIM, (split + tail) * HEAD_DIM)
    home = on_hot_half(info, out_peers(heads, tail))

    kept[...] = out[:, :, part]

    @pl.when(jnp.logical_not(home))
    def _():
        out[:, :, part] = rest[...]


def second_kernel(tail, first, count, info, temps, keys, rows, extra, _, *refs):
    queries, later, kept = (refs[at * count : (at + 1) * count] for at in range(3))
    outs, held = refs[3 * count : 4 * count], refs[-1]
    slots, tokens, _ = queries[0].shape
    heads = keys.shape[0]
    split = heads - 2 * tail
    part = slice(tail * HEAD_DIM, 2 * tail * HEAD_DIM)
    home = on_hot_half(info, out_peers(heads, tail))

    @pl.when(home)
    def _():
        for at in range(count):
            held[at] = later[at][:, :, split * HEAD_DIM :]
            outs[at][:, :, part] = extra[first + at]

    @pl.when(jnp.logical_not(home))
    def _():
        for at in range(count):
            held[at] = queries[at][:, :, (split + tail) * HEAD_DIM :]
            outs[at][:, :, part] = kept[at][...]

    places = [
        (slots, tokens, loader(held, heads - tail, at), storer(outs[at], heads - tail))
        for at in range(count)
    ]
    attend_heads(info, temps, keys, rows, places, heads - tail, heads)


def out_peers(heads, tail):
    return 2 * (heads // tail)


def on_hot_half(info, peers):
    half = peers // 2
    return (lax.axis_index("pos") >= half) == (info[info.shape[0] - 1] >= half)


def attend(kernel, name, widths, info, temps, keys, rows, refs, unread, arrays, scratch=()):
    scalars = pl.BlockSpec(memory_space=pltpu.SMEM)
    vector = pl.BlockSpec(memory_space=pltpu.VMEM)
    anywhere = pl.BlockSpec(memory_space=pl.ANY)
    leading = arrays[0].shape[:-1]
    return pl.pallas_call(
        kernel,
        in_specs=[scalars, scalars, vector, vector]
        + [vector] * len(refs)
        + [anywhere]
        + [vector] * len(arrays),
        out_specs=[vector] * len(widths),
        out_shape=[
            jax.ShapeDtypeStruct(leading + (width * HEAD_DIM,), jnp.bfloat16) for width in widths
        ],
        scratch_shapes=list(scratch),
        compiler_params=pltpu.CompilerParams(vmem_limit_bytes=16 * MIB),
        cost_estimate=cost(ATTEND_FLOPS),
        name=name,
    )(info, temps, keys, rows, *refs, unread, *arrays)


def holds(info, done):
    hot = info[info.shape[0] - 1]
    apart = jnp.bitwise_xor(lax.axis_index("pos"), hot)
    for bit in done:
        apart -= apart // (1 << bit) % 2 * (1 << bit)
    return apart == 0


def cut_kernel(stage, ways, info, *refs):
    sources, (sent, kept) = refs[: -2 * len(ways) - 1], (refs[-2 * len(ways) : -len(ways)], refs[-len(ways) :])
    for at, (start, _, order) in enumerate(ways):
        count = sent[at].shape[0]
        mine = lax.axis_index("pos") // (1 << order[stage]) % 2
        if stage:
            have = holds(info, order[: stage - 1])
            choices = [(have, sources[2 * at]), (jnp.logical_not(have), sources[2 * at + 1])]
            start = 0
        else:
            choices = [(True, sources[0])]
        for whether, source in choices:

            @pl.when(whether)
            def _():
                sent[at][...] = source[pl.ds(start + (1 - mine) * count, count)]
                kept[at][...] = source[pl.ds(start + mine * count, count)]


def cut(stage, ways, info, sources, after):
    _, positions, wide = sources[0].shape
    vector = pl.BlockSpec(memory_space=pltpu.VMEM)
    halves_of = [
        jax.ShapeDtypeStruct((count >> (stage + 1), positions, wide), sources[0].dtype)
        for _, count, _ in ways
    ]
    outs = pl.pallas_call(
        functools.partial(cut_kernel, stage, ways),
        in_specs=[pl.BlockSpec(memory_space=pltpu.SMEM)]
        + [vector] * len(sources)
        + [pl.BlockSpec(memory_space=pl.ANY)],
        out_specs=[vector] * (2 * len(ways)),
        out_shape=halves_of * 2,
        compiler_params=pltpu.CompilerParams(vmem_limit_bytes=16 * MIB),
        cost_estimate=cost(1000),
        name="cut",
    )(info, *sources, after)
    return outs[: len(ways)], outs[len(ways) :]


def extra_kernel(ways, info, temps, *refs):
    rows, near, far = refs[: 2 * len(ways)], refs[2 * len(ways) + 1], refs[2 * len(ways) + 2 : -2]
    near_out, far_out = refs[-2:]
    half, extras, tokens, wide = near.shape
    me = lax.axis_index("pos")
    live = masks(info, info.shape[0] - AHEAD + HOT, extras, tokens, rows[0].shape[1])
    live = jnp.concatenate([live] * half, 0)
    values, heats = [], []
    pieces = share_of(me, half, temps.shape[0])
    for at, ((_, _, order), (first, count)) in enumerate(zip(ways, pieces)):
        have = holds(info, order[:-1])
        for head in range(count):
            values.append(jnp.where(have, rows[2 * at][head], rows[2 * at + 1][head]))
            heats.append(temps[first + head] * (LOG2E / HEAD_DIM))
    keyed = [unit(valued.astype(jnp.float32)).astype(jnp.bfloat16).T for valued in values]
    for side in range(2):
        queries = []
        for head in range(len(values)):
            cols = slice(head * HEAD_DIM, (head + 1) * HEAD_DIM)
            query = [source[:, :, cols] for source in far] if side else [near[:, :, :, cols]]
            query = [part.astype(jnp.float32).reshape(-1, HEAD_DIM) for part in query]
            queries.append(jnp.concatenate(query, 0))
        for head, done in enumerate(softened(queries, keyed, values, heats, live)):
            cols = slice(head * HEAD_DIM, (head + 1) * HEAD_DIM)
            done = done.reshape(half, extras, tokens, HEAD_DIM).astype(jnp.bfloat16)
            (far_out if side else near_out)[:, :, :, cols] = done


def attend_extra(ways, info, temps, rows, after, near, far, wide):
    half, extras, tokens, columns = near.shape
    scalars = pl.BlockSpec(memory_space=pltpu.SMEM)
    return pl.pallas_call(
        functools.partial(extra_kernel, ways),
        grid=(1,),
        in_specs=[
            scalars,
            scalars,
        ]
        + [pl.BlockSpec(array.shape, lambda i: (0, 0, 0)) for array in rows]
        + [
            pl.BlockSpec(memory_space=pl.ANY),
            pl.BlockSpec((half, extras, tokens, wide), lambda i: (0, 0, 0, columns // wide - 1)),
        ]
        + [pl.BlockSpec((extras, tokens, wide), lambda i: (0, 0, columns // wide - 2))] * half,
        out_specs=[pl.BlockSpec((half, extras, tokens, wide), lambda i: (0, 0, 0, 0))] * 2,
        out_shape=[jax.ShapeDtypeStruct((half, extras, tokens, wide), jnp.bfloat16)] * 2,
        compiler_params=pltpu.CompilerParams(vmem_limit_bytes=16 * MIB),
        cost_estimate=cost(ATTEND_FLOPS),
        name="attend_extra",
    )(info, temps, *rows, after, near, *far)


def route(info, peers, slots, extras, rows, blocks, sites):
    me = lax.axis_index("pos")
    ahead = info.shape[0] - AHEAD
    hot_at = info.shape[0] - 1

    def clear(at, carry):
        info[at] = -1
        return carry

    lax.fori_loop(0, info.shape[0], clear, 0)
    for window in range(blocks.shape[0]):
        block = blocks[window]
        count = jnp.int32(0)
        for slot in range(HOT - 1):
            count += (info[block * HOT + slot] >= 0).astype(jnp.int32)
        info[block * HOT + count] = window

        @pl.when(count == HOT - 1)
        def _():
            info[hot_at] = block

    hot = info[hot_at]

    def offset(entry):
        window = info[entry]
        site = sites[jnp.maximum(window, 0)]
        return jnp.where(window >= 0, site - rows * (entry // HOT), rows)

    for slot in range(HOT):
        info[ahead + slot] = offset(me * HOT + slot)
    for extra in range(extras):
        info[ahead + HOT + extra] = offset(hot * HOT + slots + extra)


def paths(half, heads):
    order = tuple(range(half.bit_length() - 1))
    if heads // half % 2:
        return [(0, heads, order)]
    return [(0, heads // 2, order), (heads // 2, heads // 2, order[::-1])]


def share_of(index, half, heads):
    pieces = []
    for start, count, order in paths(half, heads):
        for bit in order:
            count //= 2
            start += index // (1 << bit) % 2 * count
        pieces.append((start, count))
    return pieces


def columns_of(piece):
    start, count = piece
    wide = count * HEAD_DIM
    if isinstance(start, int):
        return pl.ds(start * HEAD_DIM, wide)
    return pl.ds(pl.multiple_of(start * HEAD_DIM, wide), wide)


def copied(copies, sems):
    copies = [pltpu.make_async_copy(*pair, sems.at[at]) for at, pair in enumerate(copies)]
    for copy in copies:
        copy.start()
    for copy in copies:
        copy.wait()


def message(info, queries, peer, out, wide, extras, start, count, with_extras):
    slots, _, held = out.shape
    hot = info[info.shape[0] - 1]
    copies = []
    for slot in range(slots):
        window = jnp.maximum(info[peer * HOT + slot], 0)
        source = queries.at[window, :, pl.ds(start, count)]
        copies.append((source, out.at[slot, :, pl.ds(0, count)]))
    half = queries.shape[2] // wide
    for extra in range(extras if held > count else 0):
        at = 0
        for first, size in share_of(peer, half, queries.shape[2] // HEAD_DIM):
            window = info[hot * HOT + slots + extra]
            if with_extras is not None:
                window = jnp.where(with_extras, window, jnp.maximum(info[peer * HOT + extra], 0))
                first = jnp.where(with_extras, first, (start + count) // HEAD_DIM + at)
            source = queries.at[window, :, columns_of((first, size))]
            target = out.at[extra, :, pl.ds(count + at * HEAD_DIM, size * HEAD_DIM)]
            copies.append((source, target))
            at += size
    return copies


def far_copies(info, queries, steps, far, rest, wide, extras):
    half = queries.shape[2] // wide
    me = lax.axis_index("pos")
    away = jnp.logical_not(on_hot_half(info, 2 * half))
    chans = queries.shape[2]
    copies = []
    for step, out, other in zip(steps, far, rest):
        peer = jnp.bitwise_xor(me, step)
        copies += message(info, queries, peer, out, wide, extras, 0, chans - wide, away)
        copies += message(info, queries, peer, other, wide, extras, chans - wide, wide, None)
    return copies


def pack_kernel(extras, rows, wide, blocks, sites, queries, _, info, near, *refs):
    half, slots, _, _ = near.shape
    outs, (sems, blocks_held, sites_held, pair) = refs[:-4], refs[-4:]
    count = len(outs) // 2
    copied([(blocks, blocks_held), (sites, sites_held)], pair)
    route(info, 2 * half, slots, extras, rows, blocks_held, sites_held)
    base = jnp.bitwise_and(lax.axis_index("pos"), half)
    chans = queries.shape[2]
    steps = range(half, half + count)
    copies = far_copies(info, queries, steps, outs[:count], outs[count:], wide, extras)
    for at in range(half):
        copies += message(info, queries, base + at, near.at[at], wide, extras, 0, chans, None)
    copied(copies, sems)


def far_shapes(queries, slots, wide, count):
    _, tokens, chans = queries.shape
    return [jax.ShapeDtypeStruct((slots, tokens, chans), queries.dtype)] * count + [
        jax.ShapeDtypeStruct((slots, tokens, wide), queries.dtype)
    ] * count


def pack(blocks, sites, queries, tail, rows, half, slots, extras, wide, count):
    windows, tokens, chans = queries.shape
    scalars = pl.BlockSpec(memory_space=pltpu.SMEM)
    vector = pl.BlockSpec(memory_space=pltpu.VMEM)
    anywhere = pl.BlockSpec(memory_space=pl.ANY)
    info, near, *far = pl.pallas_call(
        functools.partial(pack_kernel, extras, rows, wide),
        in_specs=[anywhere] * 4,
        out_specs=[scalars] + [vector] * (1 + 2 * count),
        out_shape=[
            jax.ShapeDtypeStruct((2 * half * HOT + AHEAD,), jnp.int32),
            jax.ShapeDtypeStruct((half, slots, tokens, chans + wide), queries.dtype),
        ]
        + far_shapes(queries, slots, wide, count),
        scratch_shapes=[
            pltpu.SemaphoreType.DMA(((half + count) * (slots + 2 * extras) + count * slots,)),
            pltpu.SMEM((windows,), jnp.int32),
            pltpu.SMEM((windows,), jnp.int32),
            pltpu.SemaphoreType.DMA((2,)),
        ],
        compiler_params=pltpu.CompilerParams(vmem_limit_bytes=PACK_VMEM * MIB),
        cost_estimate=cost(PACK_FLOPS),
        name="pack",
    )(blocks, sites, queries, tail)
    return info, near, far[:count], far[count:]


def placed(info, out, sems, pieces):
    def each(act):
        at = 0
        for peer, result, start, count, column, whether in pieces:
            for slot in range(result.shape[0]):
                window = info[peer * HOT + slot]
                source = result.at[slot, :, pl.ds(start, count)]
                target = out.at[jnp.maximum(window, 0), :, pl.ds(column, count)]
                copy = pltpu.make_async_copy(source, target, sems.at[at])
                pl.when(jnp.logical_and(window >= 0, whether))(functools.partial(act, copy))
                at += 1

    each(lambda copy: copy.start())
    return lambda: each(lambda copy: copy.wait())


def unpack_early_kernel(wide, info, near, *refs):
    half = near.shape[0]
    results, (_, out, near_sems, sems) = refs[:half], refs[half:]
    me = lax.axis_index("pos")
    base = jnp.bitwise_and(me, half)
    home = on_hot_half(info, 2 * half)
    chans = out.shape[2]
    split = chans - 2 * wide
    pieces = [(base + at, near.at[at], 0, chans, 0, True) for at in range(half)]
    near_wait = placed(info, out, near_sems, pieces)
    pieces = []
    for at, result in enumerate(results):
        peer = jnp.bitwise_xor(me, half + at)
        pieces.append((peer, result, 0, split, 0, True))
        pieces.append((peer, result, split, wide, split, jnp.logical_not(home)))
    placed(info, out, sems, pieces)()
    near_wait()


def unpack_early(info, near, results, after, shape, wide):
    anywhere = pl.BlockSpec(memory_space=pl.ANY)
    half, slots, _, _ = near.shape
    return pl.pallas_call(
        functools.partial(unpack_early_kernel, wide),
        in_specs=[pl.BlockSpec(memory_space=pltpu.SMEM)]
        + [pl.BlockSpec(memory_space=pltpu.VMEM)] * (1 + half)
        + [anywhere],
        out_specs=anywhere,
        out_shape=jax.ShapeDtypeStruct(shape, near.dtype),
        scratch_shapes=[
            pltpu.SemaphoreType.DMA((half * slots,)),
            pltpu.SemaphoreType.DMA((2 * half * slots,)),
        ],
        compiler_params=pltpu.CompilerParams(vmem_limit_bytes=16 * MIB),
        cost_estimate=cost(1000),
        name="unpack_early",
    )(info, near, *results, after)


def unpack_kernel(wide, step, info, result, _, out, sems, extra_sems):
    extras = extra_sems.shape[0] // 2
    half = out.shape[2] // wide
    slots = HOT - extras
    split = out.shape[2] - 2 * wide
    peer = jnp.bitwise_xor(lax.axis_index("pos"), step)
    home = on_hot_half(info, 2 * half)
    pieces = [
        (peer, result, 0, wide, split + wide, True),
        (peer, result, wide, wide, split, home),
    ]
    wait = placed(info, out, sems, pieces)
    share = share_of(peer, half, out.shape[2] // HEAD_DIM)
    sources = [result.at[extra, :, pl.ds(wide, wide)] for extra in range(extras)]
    extra_wait = placed_extra(info, out, extra_sems, sources, share, jnp.logical_not(home))
    wait()
    extra_wait()


def placed_extra(info, out, sems, sources, share, whether):
    extras = len(sources)
    hot = info[info.shape[0] - 1]

    def each(act):
        for extra, source in enumerate(sources):
            window = info[hot * HOT + HOT - extras + extra]
            at = 0
            for place, piece in enumerate(share):
                part = source.at[:, pl.ds(at * HEAD_DIM, piece[1] * HEAD_DIM)]
                target = out.at[window, :, columns_of(piece)]
                copy = pltpu.make_async_copy(part, target, sems.at[2 * extra + place])
                pl.when(whether)(functools.partial(act, copy))
                at += piece[1]

    each(lambda copy: copy.start())
    return lambda: each(lambda copy: copy.wait())


def unpack_extra_kernel(info, near, _, out, *sems):
    half, extras, _, _ = near.shape
    home = on_hot_half(info, 2 * half)
    waits = []
    for at in range(half):
        sources = [near.at[at, extra] for extra in range(extras)]
        share = share_of(at, half, out.shape[2] // HEAD_DIM)
        waits.append(placed_extra(info, out, sems[at], sources, share, home))
    for wait in waits:
        wait()


def unpack(kernel, name, info, result, so_far, semaphores):
    anywhere = pl.BlockSpec(memory_space=pl.ANY)
    return pl.pallas_call(
        kernel,
        in_specs=[
            pl.BlockSpec(memory_space=pltpu.SMEM),
            pl.BlockSpec(memory_space=pltpu.VMEM),
            anywhere,
        ],
        out_specs=anywhere,
        out_shape=jax.ShapeDtypeStruct(so_far.shape, so_far.dtype),
        input_output_aliases={2: 0},
        scratch_shapes=[pltpu.SemaphoreType.DMA((count,)) for count in semaphores],
        compiler_params=pltpu.CompilerParams(vmem_limit_bytes=16 * MIB),
        cost_estimate=cost(UNPACK_FLOPS),
        name=name,
    )(info, result, so_far)


def exchanged(value, step):
    peers = lax.axis_size("pos")
    if step == 0:
        return value
    return lax.ppermute(value, "pos", [(i, i ^ step) for i in range(peers)])


def exchanged_near(value):
    peers = lax.axis_size("pos")
    half = peers // 2
    groups = [list(range(half)), list(range(half, peers))]
    return lax.all_to_all(value, "pos", 0, 0, axis_index_groups=groups, tiled=True)


def shards(gate_stream, key_stream, value_stream, filters, temps, queries, blocks, sites):
    rows, chans = gate_stream.shape
    taps = filters.shape[1]
    peers = lax.axis_size("pos")
    me = lax.axis_index("pos").astype(jnp.int32)
    windows = blocks.shape[0]
    heads = chans // HEAD_DIM
    extras = 2
    slots = HOT - extras
    half = peers // 2

    last = slice(rows - taps, rows)
    tail = key_stream[last].astype(jnp.float32) * value_stream[last].astype(jnp.float32)
    tail = tail.astype(jnp.bfloat16)
    earlier = lax.ppermute(tail, "pos", [(i, i + 1) for i in range(peers - 1)])
    wide = chans // half
    share = heads // half
    info, near, far, rest = pack(
        blocks, sites, queries, tail, rows, half, slots, extras, wide, half
    )
    far = [exchanged(sent, half + at) for at, sent in enumerate(far)]
    near = exchanged_near(near)
    hyena_out, valued, keyed = mix(
        gate_stream, key_stream, value_stream, earlier, filters, info
    )
    own = (info, temps, keyed, valued)

    ways = paths(half, heads)

    def halved(stage, sources, after):
        moved, kept_rows = cut(stage, ways, info, sources, after)
        pairs = []
        for (_, _, order), out, stays in zip(ways, moved, kept_rows):
            pairs += [stays, exchanged(out, 1 << order[stage])]
        return pairs, moved[0]

    def first(at, after):
        kernel = functools.partial(first_kernel, share)
        arrays = [far[at], rest[at]]
        result, back = attend(
            kernel, "attend_first", [heads - share, share], *own, [], after, arrays
        )
        sent.append(exchanged(result, half + at))
        kept.append(back)
        return result

    def second(at, count, after):
        kernel = functools.partial(second_kernel, share, at, count)
        some = slice(at, at + count)
        arrays = far[some] + sent[some] + kept[some]
        scratch = [pltpu.VMEM((count,) + kept[at].shape, jnp.bfloat16)]
        results = attend(
            kernel, "attend_second", [2 * share] * count, *own, [extra], after, arrays, scratch
        )
        late.extend(exchanged(result, half + at + more) for more, result in enumerate(results))
        return results[0]

    sent, kept, late = [], [], []
    hot_rows, after = halved(0, [valued], valued)
    after = first(0, after)
    (near_results,) = attend(near_kernel, "attend_near", [heads], *own, [], after, [near])
    near_out, after = exchanged_near(near_results), near_results
    for stage in range(1, half.bit_length() - 1):
        hot_rows, after = halved(stage, hot_rows, after)
    for at in range(1, half):
        after = first(at, after)
    near_extra, extra = attend_extra(ways, info, temps, hot_rows, after, near, far, wide)
    near_extra, after = exchanged_near(near_extra), extra
    for at in range(half):
        after = second(at, 1, after)
    so_far = unpack_early(info, near_out, sent, after, queries.shape, wide)
    kernel = unpack_extra_kernel
    so_far = unpack(kernel, "unpack_extra", info, near_extra, so_far, [2 * extras] * half)
    for at, result in enumerate(late):
        kernel = functools.partial(unpack_kernel, wide, half + at)
        so_far = unpack(kernel, "unpack", info, result, so_far, [2 * slots, 2 * extras])
    return (hyena_out, so_far)


def solution(mesh):
    placed = (
        P(("groups", "pos"), "mp"),
        P(("groups", "pos"), "mp"),
        P(("groups", "pos"), "mp"),
        P("mp", None),
        P("mp"),
        P("groups", "pos", "mp"),
        P("groups"),
        P("groups"),
    )
    return jax.shard_map(
        shards,
        mesh=mesh,
        in_specs=placed,
        out_specs=(P(("groups", "pos"), "mp"), P("groups", "pos", "mp")),
        check_vma=False,
    )
```

```python
import functools

import jax
import jax.numpy as jnp
import numpy as np
from jax import lax
from jax.experimental import pallas as pl
from jax.experimental.pallas import tpu as pltpu
from jax.sharding import PartitionSpec as P

HEAD_DIM = 128
HOT = 4
EPS = 1e-06
LOG2E = 1.4426950408889634
MIB = 1 << 20
AHEAD = 16
UNPACK_FLOPS = 20 << 30
PACK_VMEM = 60
ATTEND_FLOPS = 20 << 30
MIX_FLOPS = 100 << 30
PACK_FLOPS = 20 << 30


def cost(flops):
    return pl.CostEstimate(flops=flops, bytes_accessed=1000, transcendentals=0)


def halves(array):
    high = array.astype(jnp.bfloat16)
    low = (array - high.astype(jnp.float32)).astype(jnp.bfloat16)
    return high, low


def transforms(taps):
    size = 2 * taps
    odd = 2 * np.arange(taps) + 1
    angle = np.pi / size * ((odd[:, None] * np.arange(size)[None, :]) % (2 * size))
    forward = np.concatenate([np.cos(angle), -np.sin(angle)], 0)
    inverse = forward.T[taps:] * (2.0 / size)
    out = []
    for matrix in (forward, inverse):
        high = matrix.astype(jnp.bfloat16)
        low = (matrix - high.astype(np.float64)).astype(jnp.bfloat16)
        out.append(np.concatenate([high, low], 0))
    return out


def unit(block):
    return block * lax.rsqrt(jnp.mean(block * block, axis=-1, keepdims=True) + EPS)


def mix_rows(starts, before, gate, key, value, filters, forward, inverse, out, rows_of, keys_of):
    _, wide = gate.shape
    taps = filters.shape[1]
    size = 2 * taps
    f32 = jnp.float32
    fwd = forward[...]
    inv = inverse[...]
    high, low = halves(filters[...])
    across = (((1,), (1,)), ((), ()))
    both = lax.dot_general(fwd[:, :taps], high, across, preferred_element_type=f32)
    spectrum = both[:size] + both[size:]
    spectrum += lax.dot_general(fwd[:size, :taps], low, across, preferred_element_type=f32)
    hr, hi = spectrum[:taps], spectrum[taps:]
    for start in starts:
        part = slice(start, start + taps)
        now = products(key, value, part)
        both = jnp.dot(fwd, jnp.concatenate([before, now], 0), preferred_element_type=f32)
        seen = both[:size] + both[size:]
        xr, xi = seen[:taps], seen[taps:]
        product = jnp.concatenate([xr * hr - xi * hi, xr * hi + xi * hr], 0)
        high, low = halves(product)
        both = jnp.dot(inv, high, preferred_element_type=f32)
        mixed = both[:taps] + both[taps:]
        mixed += jnp.dot(inv[:taps], low, preferred_element_type=f32)
        result = (gate[part, :].astype(f32) * mixed).astype(jnp.bfloat16)
        out[part, :] = result
        for head in range(wide // HEAD_DIM):
            piece = result[:, head * HEAD_DIM : (head + 1) * HEAD_DIM]
            rows_of[head, part, :] = piece
            keys_of[head, :, part] = unit(piece.astype(f32)).astype(jnp.bfloat16).T
        before = now


def products(key, value, part):
    return (key[part, :].astype(jnp.float32) * value[part, :].astype(jnp.float32)).astype(jnp.bfloat16)


def mix_later_kernel(gate, key, value, filters, forward, inverse, _, *outs):
    taps = filters.shape[1]
    before = products(key, value, slice(0, taps))
    starts = range(taps, gate.shape[0], taps)
    mix_rows(starts, before, gate, key, value, filters, forward, inverse, *outs)


def mix_first_kernel(gate, key, value, filters, forward, inverse, earlier, *refs):
    mix_rows([0], earlier[...], gate, key, value, filters, forward, inverse, *refs[-3:])


def mix(gate, key, value, earlier, filters, after):
    rows, chans = gate.shape
    taps = filters.shape[1]
    heads = chans // HEAD_DIM
    wide = 8 * HEAD_DIM
    forward, inverse = (jnp.asarray(matrix) for matrix in transforms(taps))
    anywhere = pl.BlockSpec(memory_space=pl.ANY)
    whole = lambda array: pl.BlockSpec(array.shape, lambda i: (0, 0))
    first = pl.BlockSpec((taps, wide), lambda i: (0, i))

    def specs(high):
        stream = pl.BlockSpec((high, wide), lambda i: (0, i))
        by_head = pl.BlockSpec((wide // HEAD_DIM, high, HEAD_DIM), lambda i: (i, 0, 0))
        turned = pl.BlockSpec((wide // HEAD_DIM, HEAD_DIM, high), lambda i: (i, 0, 0))
        weights = pl.BlockSpec((wide, taps), lambda i: (i, 0))
        return [stream] * 3 + [weights, whole(forward), whole(inverse)], [stream, by_head, turned]

    params = dict(
        grid=(chans // wide,),
        out_shape=[
            jax.ShapeDtypeStruct((rows, chans), jnp.bfloat16),
            jax.ShapeDtypeStruct((heads, rows, HEAD_DIM), jnp.bfloat16),
            jax.ShapeDtypeStruct((heads, HEAD_DIM, rows), jnp.bfloat16),
        ],
        compiler_params=pltpu.CompilerParams(vmem_limit_bytes=24 * MIB),
        cost_estimate=cost(MIX_FLOPS),
    )
    arrays = (gate, key, value, filters, forward, inverse)
    ins, outs = specs(rows)
    mixed = pl.pallas_call(
        mix_later_kernel, in_specs=ins + [anywhere], out_specs=outs, name="mix_later", **params
    )(*arrays, after)
    ins, outs = specs(taps)
    return pl.pallas_call(
        mix_first_kernel,
        in_specs=ins + [first] + [anywhere] * 3,
        out_specs=outs,
        input_output_aliases={7: 0, 8: 1, 9: 2},
        name="mix_first",
        **params,
    )(*arrays, earlier, *mixed)


def softened(queries, keys, rows, heats, live):
    f32 = jnp.float32
    queries = [unit(query).astype(jnp.bfloat16) for query in queries]
    scores = [jnp.dot(*pair, preferred_element_type=f32) for pair in zip(queries, keys)]
    weights = [jnp.where(live, jnp.exp2(s * heat), 0.0) for s, heat in zip(scores, heats)]
    totals = [jnp.sum(weight, axis=-1, keepdims=True) for weight in weights]
    sums = [
        jnp.dot(weight.astype(jnp.bfloat16), rows_of, preferred_element_type=f32)
        for weight, rows_of in zip(weights, rows)
    ]
    return [part / total for part, total in zip(sums, totals)]


def together(count, high):
    most = 8 if high <= 128 else 4
    return max(size for size in range(1, most + 1) if count % size == 0)


def masks(offsets, first, slots, tokens, positions):
    place = lax.broadcasted_iota(jnp.int32, (tokens, positions), 1)
    return jnp.concatenate([place < offsets[first + slot] for slot in range(slots)], 0)


def attend_heads(info, temps, keys, rows, places, first, last):
    positions = keys.shape[2]
    slots, tokens = places[0][:2]
    each = slots * tokens
    live = masks(info, info.shape[0] - AHEAD, slots, tokens, positions)
    live = jnp.concatenate([live] * len(places), 0)

    batch = together(last - first, each * len(places))

    def some(step, carry):
        heads = [first + step * batch + at for at in range(batch)]
        queries = []
        for head in heads:
            parts = [load(head).astype(jnp.float32) for _, _, load, _ in places]
            queries.append(jnp.concatenate([part.reshape(each, HEAD_DIM) for part in parts], 0))
        heats = [temps[head] * (LOG2E / HEAD_DIM) for head in heads]
        done = softened(queries, [keys[h] for h in heads], [rows[h] for h in heads], heats, live)
        for head, block in zip(heads, done):
            for place, (_, _, _, store) in enumerate(places):
                part = block[place * each : (place + 1) * each].reshape(slots, tokens, HEAD_DIM)
                store(head, part.astype(jnp.bfloat16))
        return carry

    lax.fori_loop(0, (last - first) // batch, some, 0)


def columns(head):
    return pl.ds(pl.multiple_of(head * HEAD_DIM, HEAD_DIM), HEAD_DIM)


def loader(ref, shift, *at):
    return lambda head: ref[at + (slice(None), slice(None), columns(head - shift))]


def storer(ref, shift, *at):
    def store(head, block):
        ref[at + (slice(None), slice(None), columns(head - shift))] = block

    return store


def near_kernel(info, temps, keys, rows, _, near, out):
    half, slots, tokens, _ = near.shape
    places = [(slots, tokens, loader(near, 0, at), storer(out, 0, at)) for at in range(half)]
    attend_heads(info, temps, keys, rows, places, 0, keys.shape[0])


def first_kernel(tail, info, temps, keys, rows, _, queries, rest, out, kept):
    slots, tokens, _ = queries.shape
    heads = keys.shape[0]
    split = heads - 2 * tail
    places = [(slots, tokens, loader(queries, 0), storer(out, 0))]
    attend_heads(info, temps, keys, rows, places, 0, heads - tail)
    part = slice(split * HEAD_DIM, (split + tail) * HEAD_DIM)
    home = on_hot_half(info, out_peers(heads, tail))

    kept[...] = out[:, :, part]

    @pl.when(jnp.logical_not(home))
    def _():
        out[:, :, part] = rest[...]


def second_kernel(tail, first, count, info, temps, keys, rows, extra, _, *refs):
    queries, later, kept = (refs[at * count : (at + 1) * count] for at in range(3))
    outs, held = refs[3 * count : 4 * count], refs[-1]
    slots, tokens, _ = queries[0].shape
    heads = keys.shape[0]
    split = heads - 2 * tail
    part = slice(tail * HEAD_DIM, 2 * tail * HEAD_DIM)
    home = on_hot_half(info, out_peers(heads, tail))

    @pl.when(home)
    def _():
        for at in range(count):
            held[at] = later[at][:, :, split * HEAD_DIM :]
            outs[at][:, :, part] = extra[first + at]

    @pl.when(jnp.logical_not(home))
    def _():
        for at in range(count):
            held[at] = queries[at][:, :, (split + tail) * HEAD_DIM :]
            outs[at][:, :, part] = kept[at][...]

    places = [
        (slots, tokens, loader(held, heads - tail, at), storer(outs[at], heads - tail))
        for at in range(count)
    ]
    attend_heads(info, temps, keys, rows, places, heads - tail, heads)


def out_peers(heads, tail):
    return 2 * (heads // tail)


def on_hot_half(info, peers):
    half = peers // 2
    return (lax.axis_index("pos") >= half) == (info[info.shape[0] - 1] >= half)


def attend(kernel, name, widths, info, temps, keys, rows, refs, unread, arrays, scratch=()):
    scalars = pl.BlockSpec(memory_space=pltpu.SMEM)
    vector = pl.BlockSpec(memory_space=pltpu.VMEM)
    anywhere = pl.BlockSpec(memory_space=pl.ANY)
    leading = arrays[0].shape[:-1]
    return pl.pallas_call(
        kernel,
        in_specs=[scalars, scalars, vector, vector]
        + [vector] * len(refs)
        + [anywhere]
        + [vector] * len(arrays),
        out_specs=[vector] * len(widths),
        out_shape=[
            jax.ShapeDtypeStruct(leading + (width * HEAD_DIM,), jnp.bfloat16) for width in widths
        ],
        scratch_shapes=list(scratch),
        compiler_params=pltpu.CompilerParams(vmem_limit_bytes=16 * MIB),
        cost_estimate=cost(ATTEND_FLOPS),
        name=name,
    )(info, temps, keys, rows, *refs, unread, *arrays)


def holds(info, done):
    hot = info[info.shape[0] - 1]
    apart = jnp.bitwise_xor(lax.axis_index("pos"), hot)
    for bit in done:
        apart -= apart // (1 << bit) % 2 * (1 << bit)
    return apart == 0


def cut_kernel(stage, ways, info, *refs):
    sources, (sent, kept) = refs[: -2 * len(ways) - 1], (refs[-2 * len(ways) : -len(ways)], refs[-len(ways) :])
    for at, (start, _, order) in enumerate(ways):
        count = sent[at].shape[0]
        mine = lax.axis_index("pos") // (1 << order[stage]) % 2
        if stage:
            have = holds(info, order[: stage - 1])
            choices = [(have, sources[2 * at]), (jnp.logical_not(have), sources[2 * at + 1])]
            start = 0
        else:
            choices = [(True, sources[0])]
        for whether, source in choices:

            @pl.when(whether)
            def _():
                sent[at][...] = source[pl.ds(start + (1 - mine) * count, count)]
                kept[at][...] = source[pl.ds(start + mine * count, count)]


def cut(stage, ways, info, sources, after):
    _, positions, wide = sources[0].shape
    vector = pl.BlockSpec(memory_space=pltpu.VMEM)
    halves_of = [
        jax.ShapeDtypeStruct((count >> (stage + 1), positions, wide), sources[0].dtype)
        for _, count, _ in ways
    ]
    outs = pl.pallas_call(
        functools.partial(cut_kernel, stage, ways),
        in_specs=[pl.BlockSpec(memory_space=pltpu.SMEM)]
        + [vector] * len(sources)
        + [pl.BlockSpec(memory_space=pl.ANY)],
        out_specs=[vector] * (2 * len(ways)),
        out_shape=halves_of * 2,
        compiler_params=pltpu.CompilerParams(vmem_limit_bytes=16 * MIB),
        cost_estimate=cost(1000),
        name="cut",
    )(info, *sources, after)
    return outs[: len(ways)], outs[len(ways) :]


def extra_kernel(ways, info, temps, *refs):
    rows, near, far = refs[: 2 * len(ways)], refs[2 * len(ways) + 1], refs[2 * len(ways) + 2 : -2]
    near_out, far_out = refs[-2:]
    half, extras, tokens, wide = near.shape
    me = lax.axis_index("pos")
    live = masks(info, info.shape[0] - AHEAD + HOT, extras, tokens, rows[0].shape[1])
    live = jnp.concatenate([live] * half, 0)
    values, heats = [], []
    pieces = share_of(me, half, temps.shape[0])
    for at, ((_, _, order), (first, count)) in enumerate(zip(ways, pieces)):
        have = holds(info, order[:-1])
        for head in range(count):
            values.append(jnp.where(have, rows[2 * at][head], rows[2 * at + 1][head]))
            heats.append(temps[first + head] * (LOG2E / HEAD_DIM))
    keyed = [unit(valued.astype(jnp.float32)).astype(jnp.bfloat16).T for valued in values]
    for side in range(2):
        queries = []
        for head in range(len(values)):
            cols = slice(head * HEAD_DIM, (head + 1) * HEAD_DIM)
            query = [source[:, :, cols] for source in far] if side else [near[:, :, :, cols]]
            query = [part.astype(jnp.float32).reshape(-1, HEAD_DIM) for part in query]
            queries.append(jnp.concatenate(query, 0))
        for head, done in enumerate(softened(queries, keyed, values, heats, live)):
            cols = slice(head * HEAD_DIM, (head + 1) * HEAD_DIM)
            done = done.reshape(half, extras, tokens, HEAD_DIM).astype(jnp.bfloat16)
            (far_out if side else near_out)[:, :, :, cols] = done


def attend_extra(ways, info, temps, rows, after, near, far, wide):
    half, extras, tokens, columns = near.shape
    scalars = pl.BlockSpec(memory_space=pltpu.SMEM)
    return pl.pallas_call(
        functools.partial(extra_kernel, ways),
        grid=(1,),
        in_specs=[
            scalars,
            scalars,
        ]
        + [pl.BlockSpec(array.shape, lambda i: (0, 0, 0)) for array in rows]
        + [
            pl.BlockSpec(memory_space=pl.ANY),
            pl.BlockSpec((half, extras, tokens, wide), lambda i: (0, 0, 0, columns // wide - 1)),
        ]
        + [pl.BlockSpec((extras, tokens, wide), lambda i: (0, 0, columns // wide - 2))] * half,
        out_specs=[pl.BlockSpec((half, extras, tokens, wide), lambda i: (0, 0, 0, 0))] * 2,
        out_shape=[jax.ShapeDtypeStruct((half, extras, tokens, wide), jnp.bfloat16)] * 2,
        compiler_params=pltpu.CompilerParams(vmem_limit_bytes=16 * MIB),
        cost_estimate=cost(ATTEND_FLOPS),
        name="attend_extra",
    )(info, temps, *rows, after, near, *far)


def route(info, peers, slots, extras, rows, blocks, sites):
    me = lax.axis_index("pos")
    ahead = info.shape[0] - AHEAD
    hot_at = info.shape[0] - 1

    def clear(at, carry):
        info[at] = -1
        return carry

    lax.fori_loop(0, info.shape[0], clear, 0)
    for window in range(blocks.shape[0]):
        block = blocks[window]
        count = jnp.int32(0)
        for slot in range(HOT - 1):
            count += (info[block * HOT + slot] >= 0).astype(jnp.int32)
        info[block * HOT + count] = window

        @pl.when(count == HOT - 1)
        def _():
            info[hot_at] = block

    hot = info[hot_at]

    def offset(entry):
        window = info[entry]
        site = sites[jnp.maximum(window, 0)]
        return jnp.where(window >= 0, site - rows * (entry // HOT), rows)

    for slot in range(HOT):
        info[ahead + slot] = offset(me * HOT + slot)
    for extra in range(extras):
        info[ahead + HOT + extra] = offset(hot * HOT + slots + extra)


def paths(half, heads):
    order = tuple(range(half.bit_length() - 1))
    if heads // half % 2:
        return [(0, heads, order)]
    return [(0, heads // 2, order), (heads // 2, heads // 2, order[::-1])]


def share_of(index, half, heads):
    pieces = []
    for start, count, order in paths(half, heads):
        for bit in order:
            count //= 2
            start += index // (1 << bit) % 2 * count
        pieces.append((start, count))
    return pieces


def columns_of(piece):
    start, count = piece
    wide = count * HEAD_DIM
    if isinstance(start, int):
        return pl.ds(start * HEAD_DIM, wide)
    return pl.ds(pl.multiple_of(start * HEAD_DIM, wide), wide)


def copied(copies, sems):
    copies = [pltpu.make_async_copy(*pair, sems.at[at]) for at, pair in enumerate(copies)]
    for copy in copies:
        copy.start()
    for copy in copies:
        copy.wait()


def message(info, queries, peer, out, wide, extras, start, count, with_extras):
    slots, _, held = out.shape
    hot = info[info.shape[0] - 1]
    copies = []
    for slot in range(slots):
        window = jnp.maximum(info[peer * HOT + slot], 0)
        source = queries.at[window, :, pl.ds(start, count)]
        copies.append((source, out.at[slot, :, pl.ds(0, count)]))
    half = queries.shape[2] // wide
    for extra in range(extras if held > count else 0):
        at = 0
        for first, size in share_of(peer, half, queries.shape[2] // HEAD_DIM):
            window = info[hot * HOT + slots + extra]
            if with_extras is not None:
                window = jnp.where(with_extras, window, jnp.maximum(info[peer * HOT + extra], 0))
                first = jnp.where(with_extras, first, (start + count) // HEAD_DIM + at)
            source = queries.at[window, :, columns_of((first, size))]
            target = out.at[extra, :, pl.ds(count + at * HEAD_DIM, size * HEAD_DIM)]
            copies.append((source, target))
            at += size
    return copies


def far_steps(half):
    return [half + at for at in (*range(half // 2, half), *range(half // 2))]


def far_copies(info, queries, steps, far, rest, wide, extras):
    half = queries.shape[2] // wide
    me = lax.axis_index("pos")
    away = jnp.logical_not(on_hot_half(info, 2 * half))
    chans = queries.shape[2]
    copies = []
    for step, out, other in zip(steps, far, rest):
        peer = jnp.bitwise_xor(me, step)
        copies += message(info, queries, peer, out, wide, extras, 0, chans - wide, away)
        copies += message(info, queries, peer, other, wide, extras, chans - wide, wide, None)
    return copies


def pack_kernel(extras, rows, wide, blocks, sites, queries, _, info, near, *refs):
    half, slots, _, _ = near.shape
    outs, (sems, blocks_held, sites_held, pair) = refs[:-4], refs[-4:]
    count = len(outs) // 2
    copied([(blocks, blocks_held), (sites, sites_held)], pair)
    route(info, 2 * half, slots, extras, rows, blocks_held, sites_held)
    base = jnp.bitwise_and(lax.axis_index("pos"), half)
    chans = queries.shape[2]
    steps = far_steps(half)
    copies = far_copies(info, queries, steps, outs[:count], outs[count:], wide, extras)
    for at in range(half):
        copies += message(info, queries, base + at, near.at[at], wide, extras, 0, chans, None)
    copied(copies, sems)


def far_shapes(queries, slots, wide, count):
    _, tokens, chans = queries.shape
    return [jax.ShapeDtypeStruct((slots, tokens, chans), queries.dtype)] * count + [
        jax.ShapeDtypeStruct((slots, tokens, wide), queries.dtype)
    ] * count


def pack(blocks, sites, queries, tail, rows, half, slots, extras, wide, count):
    windows, tokens, chans = queries.shape
    scalars = pl.BlockSpec(memory_space=pltpu.SMEM)
    vector = pl.BlockSpec(memory_space=pltpu.VMEM)
    anywhere = pl.BlockSpec(memory_space=pl.ANY)
    info, near, *far = pl.pallas_call(
        functools.partial(pack_kernel, extras, rows, wide),
        in_specs=[anywhere] * 4,
        out_specs=[scalars] + [vector] * (1 + 2 * count),
        out_shape=[
            jax.ShapeDtypeStruct((2 * half * HOT + AHEAD,), jnp.int32),
            jax.ShapeDtypeStruct((half, slots, tokens, chans + wide), queries.dtype),
        ]
        + far_shapes(queries, slots, wide, count),
        scratch_shapes=[
            pltpu.SemaphoreType.DMA(((half + count) * (slots + 2 * extras) + count * slots,)),
            pltpu.SMEM((windows,), jnp.int32),
            pltpu.SMEM((windows,), jnp.int32),
            pltpu.SemaphoreType.DMA((2,)),
        ],
        compiler_params=pltpu.CompilerParams(vmem_limit_bytes=PACK_VMEM * MIB),
        cost_estimate=cost(PACK_FLOPS),
        name="pack",
    )(blocks, sites, queries, tail)
    return info, near, far[:count], far[count:]


def placed(info, out, sems, pieces):
    def each(act):
        at = 0
        for peer, result, start, count, column, whether in pieces:
            for slot in range(result.shape[0]):
                window = info[peer * HOT + slot]
                source = result.at[slot, :, pl.ds(start, count)]
                target = out.at[jnp.maximum(window, 0), :, pl.ds(column, count)]
                copy = pltpu.make_async_copy(source, target, sems.at[at])
                pl.when(jnp.logical_and(window >= 0, whether))(functools.partial(act, copy))
                at += 1

    each(lambda copy: copy.start())
    return lambda: each(lambda copy: copy.wait())


def unpack_early_kernel(wide, info, near, *refs):
    half = near.shape[0]
    results, (_, out, near_sems, sems) = refs[:half], refs[half:]
    me = lax.axis_index("pos")
    base = jnp.bitwise_and(me, half)
    home = on_hot_half(info, 2 * half)
    chans = out.shape[2]
    split = chans - 2 * wide
    pieces = [(base + at, near.at[at], 0, chans, 0, True) for at in range(half)]
    near_wait = placed(info, out, near_sems, pieces)
    pieces = []
    for at, result in enumerate(results):
        peer = jnp.bitwise_xor(me, far_steps(half)[at])
        pieces.append((peer, result, 0, split, 0, True))
        pieces.append((peer, result, split, wide, split, jnp.logical_not(home)))
    placed(info, out, sems, pieces)()
    near_wait()


def unpack_early(info, near, results, after, shape, wide):
    anywhere = pl.BlockSpec(memory_space=pl.ANY)
    half, slots, _, _ = near.shape
    return pl.pallas_call(
        functools.partial(unpack_early_kernel, wide),
        in_specs=[pl.BlockSpec(memory_space=pltpu.SMEM)]
        + [pl.BlockSpec(memory_space=pltpu.VMEM)] * (1 + half)
        + [anywhere],
        out_specs=anywhere,
        out_shape=jax.ShapeDtypeStruct(shape, near.dtype),
        scratch_shapes=[
            pltpu.SemaphoreType.DMA((half * slots,)),
            pltpu.SemaphoreType.DMA((2 * half * slots,)),
        ],
        compiler_params=pltpu.CompilerParams(vmem_limit_bytes=16 * MIB),
        cost_estimate=cost(1000),
        name="unpack_early",
    )(info, near, *results, after)


def unpack_kernel(wide, steps, info, *refs):
    results, out, semaphores = refs[: len(steps)], refs[len(steps) + 1], refs[len(steps) + 2 :]
    half = out.shape[2] // wide
    split = out.shape[2] - 2 * wide
    home = on_hot_half(info, 2 * half)
    waits = []
    for step, result, sems, extra_sems in zip(steps, results, semaphores[::2], semaphores[1::2]):
        extras = extra_sems.shape[0] // 2
        peer = jnp.bitwise_xor(lax.axis_index("pos"), step)
        pieces = [
            (peer, result, 0, wide, split + wide, True),
            (peer, result, wide, wide, split, home),
        ]
        waits.append(placed(info, out, sems, pieces))
        share = share_of(peer, half, out.shape[2] // HEAD_DIM)
        sources = [result.at[extra, :, pl.ds(wide, wide)] for extra in range(extras)]
        away = jnp.logical_not(home)
        waits.append(placed_extra(info, out, extra_sems, sources, share, away))
    for wait in waits:
        wait()


def placed_extra(info, out, sems, sources, share, whether):
    extras = len(sources)
    hot = info[info.shape[0] - 1]

    def each(act):
        for extra, source in enumerate(sources):
            window = info[hot * HOT + HOT - extras + extra]
            at = 0
            for place, piece in enumerate(share):
                part = source.at[:, pl.ds(at * HEAD_DIM, piece[1] * HEAD_DIM)]
                target = out.at[window, :, columns_of(piece)]
                copy = pltpu.make_async_copy(part, target, sems.at[2 * extra + place])
                pl.when(whether)(functools.partial(act, copy))
                at += piece[1]

    each(lambda copy: copy.start())
    return lambda: each(lambda copy: copy.wait())


def unpack_extra_kernel(info, near, _, out, *sems):
    half, extras, _, _ = near.shape
    home = on_hot_half(info, 2 * half)
    waits = []
    for at in range(half):
        sources = [near.at[at, extra] for extra in range(extras)]
        share = share_of(at, half, out.shape[2] // HEAD_DIM)
        waits.append(placed_extra(info, out, sems[at], sources, share, home))
    for wait in waits:
        wait()


def unpack(kernel, name, info, results, so_far, semaphores):
    anywhere = pl.BlockSpec(memory_space=pl.ANY)
    vector = pl.BlockSpec(memory_space=pltpu.VMEM)
    return pl.pallas_call(
        kernel,
        in_specs=[pl.BlockSpec(memory_space=pltpu.SMEM)] + [vector] * len(results) + [anywhere],
        out_specs=anywhere,
        out_shape=jax.ShapeDtypeStruct(so_far.shape, so_far.dtype),
        input_output_aliases={1 + len(results): 0},
        scratch_shapes=[pltpu.SemaphoreType.DMA((count,)) for count in semaphores],
        compiler_params=pltpu.CompilerParams(vmem_limit_bytes=16 * MIB),
        cost_estimate=cost(UNPACK_FLOPS),
        name=name,
    )(info, *results, so_far)


def exchanged(value, step):
    peers = lax.axis_size("pos")
    if step == 0:
        return value
    return lax.ppermute(value, "pos", [(i, i ^ step) for i in range(peers)])


def exchanged_near(value):
    peers = lax.axis_size("pos")
    half = peers // 2
    groups = [list(range(half)), list(range(half, peers))]
    return lax.all_to_all(value, "pos", 0, 0, axis_index_groups=groups, tiled=True)


def shards(gate_stream, key_stream, value_stream, filters, temps, queries, blocks, sites):
    rows, chans = gate_stream.shape
    taps = filters.shape[1]
    peers = lax.axis_size("pos")
    me = lax.axis_index("pos").astype(jnp.int32)
    windows = blocks.shape[0]
    heads = chans // HEAD_DIM
    extras = 2
    slots = HOT - extras
    half = peers // 2

    last = slice(rows - taps, rows)
    tail = key_stream[last].astype(jnp.float32) * value_stream[last].astype(jnp.float32)
    tail = tail.astype(jnp.bfloat16)
    earlier = lax.ppermute(tail, "pos", [(i, i + 1) for i in range(peers - 1)])
    wide = chans // half
    share = heads // half
    info, near, far, rest = pack(
        blocks, sites, queries, tail, rows, half, slots, extras, wide, half
    )
    far = [exchanged(sent, step) for step, sent in zip(far_steps(half), far)]
    near = exchanged_near(near)
    hyena_out, valued, keyed = mix(
        gate_stream, key_stream, value_stream, earlier, filters, info
    )
    own = (info, temps, keyed, valued)

    ways = paths(half, heads)

    def halved(stage, sources, after):
        moved, kept_rows = cut(stage, ways, info, sources, after)
        pairs = []
        for (_, _, order), out, stays in zip(ways, moved, kept_rows):
            pairs += [stays, exchanged(out, 1 << order[stage])]
        return pairs, moved[0]

    def first(at, after):
        kernel = functools.partial(first_kernel, share)
        arrays = [far[at], rest[at]]
        result, back = attend(
            kernel, "attend_first", [heads - share, share], *own, [], after, arrays
        )
        sent.append(exchanged(result, far_steps(half)[at]))
        kept.append(back)
        return result

    def second(at, count, after):
        kernel = functools.partial(second_kernel, share, at, count)
        some = slice(at, at + count)
        arrays = far[some] + sent[some] + kept[some]
        scratch = [pltpu.VMEM((count,) + kept[at].shape, jnp.bfloat16)]
        results = attend(
            kernel, "attend_second", [2 * share] * count, *own, [extra], after, arrays, scratch
        )
        late.extend(
            exchanged(result, far_steps(half)[at + more]) for more, result in enumerate(results)
        )
        return results[0]

    sent, kept, late = [], [], []
    hot_rows, after = halved(0, [valued], valued)
    after = first(0, after)
    (near_results,) = attend(near_kernel, "attend_near", [heads], *own, [], after, [near])
    near_out, after = exchanged_near(near_results), near_results
    for stage in range(1, half.bit_length() - 1):
        hot_rows, after = halved(stage, hot_rows, after)
    for at in range(1, half):
        after = first(at, after)
    near_extra, extra = attend_extra(ways, info, temps, hot_rows, after, near, far, wide)
    near_extra, after = exchanged_near(near_extra), extra
    for at in range(half):
        after = second(at, 1, after)
    so_far = unpack_early(info, near_out, sent, after, queries.shape, wide)
    count = [2 * extras] * half
    so_far = unpack(unpack_extra_kernel, "unpack_extra", info, [near_extra], so_far, count)
    for at in range(0, half, 2):
        kernel = functools.partial(unpack_kernel, wide, far_steps(half)[at : at + 2])
        results = late[at : at + 2]
        so_far = unpack(kernel, "unpack", info, results, so_far, [2 * slots, 2 * extras] * 2)
    return (hyena_out, so_far)


def solution(mesh):
    placed = (
        P(("groups", "pos"), "mp"),
        P(("groups", "pos"), "mp"),
        P(("groups", "pos"), "mp"),
        P("mp", None),
        P("mp"),
        P("groups", "pos", "mp"),
        P("groups"),
        P("groups"),
    )
    return jax.shard_map(
        shards,
        mesh=mesh,
        in_specs=placed,
        out_specs=(P(("groups", "pos"), "mp"), P("groups", "pos", "mp")),
        check_vma=False,
    )
```

```python
import functools

import jax
import jax.numpy as jnp
import numpy as np
from jax import lax
from jax.experimental import pallas as pl
from jax.experimental.pallas import tpu as pltpu
from jax.sharding import PartitionSpec as P

HEAD_DIM = 128
HOT = 4
EPS = 1e-06
LOG2E = 1.4426950408889634
MIB = 1 << 20
AHEAD = 16
UNPACK_FLOPS = 20 << 30
PACK_VMEM = 60
ATTEND_FLOPS = 20 << 30
MIX_FLOPS = 100 << 30
PACK_FLOPS = 20 << 30


def cost(flops):
    return pl.CostEstimate(flops=flops, bytes_accessed=1000, transcendentals=0)


def halves(array):
    high = array.astype(jnp.bfloat16)
    low = (array - high.astype(jnp.float32)).astype(jnp.bfloat16)
    return high, low


def transforms(taps):
    size = 2 * taps
    odd = 2 * np.arange(taps) + 1
    angle = np.pi / size * ((odd[:, None] * np.arange(size)[None, :]) % (2 * size))
    forward = np.concatenate([np.cos(angle), -np.sin(angle)], 0)
    inverse = forward.T[taps:] * (2.0 / size)
    out = []
    for matrix in (forward, inverse):
        high = matrix.astype(jnp.bfloat16)
        low = (matrix - high.astype(np.float64)).astype(jnp.bfloat16)
        out.append(np.concatenate([high, low], 0))
    return out


def unit(block):
    return block * lax.rsqrt(jnp.mean(block * block, axis=-1, keepdims=True) + EPS)


def mix_rows(starts, before, gate, key, value, filters, forward, inverse, out, rows_of, keys_of):
    _, wide = gate.shape
    taps = filters.shape[1]
    size = 2 * taps
    f32 = jnp.float32
    fwd = forward[...]
    inv = inverse[...]
    high, low = halves(filters[...])
    across = (((1,), (1,)), ((), ()))
    both = lax.dot_general(fwd[:, :taps], high, across, preferred_element_type=f32)
    spectrum = both[:size] + both[size:]
    spectrum += lax.dot_general(fwd[:size, :taps], low, across, preferred_element_type=f32)
    hr, hi = spectrum[:taps], spectrum[taps:]
    for start in starts:
        part = slice(start, start + taps)
        now = products(key, value, part)
        both = jnp.dot(fwd, jnp.concatenate([before, now], 0), preferred_element_type=f32)
        seen = both[:size] + both[size:]
        xr, xi = seen[:taps], seen[taps:]
        product = jnp.concatenate([xr * hr - xi * hi, xr * hi + xi * hr], 0)
        high, low = halves(product)
        both = jnp.dot(inv, high, preferred_element_type=f32)
        mixed = both[:taps] + both[taps:]
        mixed += jnp.dot(inv[:taps], low, preferred_element_type=f32)
        result = (gate[part, :].astype(f32) * mixed).astype(jnp.bfloat16)
        out[part, :] = result
        for head in range(wide // HEAD_DIM):
            piece = result[:, head * HEAD_DIM : (head + 1) * HEAD_DIM]
            rows_of[head, part, :] = piece
            keys_of[head, :, part] = unit(piece.astype(f32)).astype(jnp.bfloat16).T
        before = now


def products(key, value, part):
    return (key[part, :].astype(jnp.float32) * value[part, :].astype(jnp.float32)).astype(jnp.bfloat16)


def mix_later_kernel(gate, key, value, filters, forward, inverse, _, *outs):
    taps = filters.shape[1]
    before = products(key, value, slice(0, taps))
    starts = range(taps, gate.shape[0], taps)
    mix_rows(starts, before, gate, key, value, filters, forward, inverse, *outs)


def mix_first_kernel(gate, key, value, filters, forward, inverse, earlier, *refs):
    mix_rows([0], earlier[...], gate, key, value, filters, forward, inverse, *refs[-3:])


def mix(gate, key, value, earlier, filters, after):
    rows, chans = gate.shape
    taps = filters.shape[1]
    heads = chans // HEAD_DIM
    wide = 8 * HEAD_DIM
    forward, inverse = (jnp.asarray(matrix) for matrix in transforms(taps))
    anywhere = pl.BlockSpec(memory_space=pl.ANY)
    whole = lambda array: pl.BlockSpec(array.shape, lambda i: (0, 0))
    first = pl.BlockSpec((taps, wide), lambda i: (0, i))

    def specs(high):
        stream = pl.BlockSpec((high, wide), lambda i: (0, i))
        by_head = pl.BlockSpec((wide // HEAD_DIM, high, HEAD_DIM), lambda i: (i, 0, 0))
        turned = pl.BlockSpec((wide // HEAD_DIM, HEAD_DIM, high), lambda i: (i, 0, 0))
        weights = pl.BlockSpec((wide, taps), lambda i: (i, 0))
        return [stream] * 3 + [weights, whole(forward), whole(inverse)], [stream, by_head, turned]

    params = dict(
        grid=(chans // wide,),
        out_shape=[
            jax.ShapeDtypeStruct((rows, chans), jnp.bfloat16),
            jax.ShapeDtypeStruct((heads, rows, HEAD_DIM), jnp.bfloat16),
            jax.ShapeDtypeStruct((heads, HEAD_DIM, rows), jnp.bfloat16),
        ],
        compiler_params=pltpu.CompilerParams(vmem_limit_bytes=24 * MIB),
        cost_estimate=cost(MIX_FLOPS),
    )
    arrays = (gate, key, value, filters, forward, inverse)
    ins, outs = specs(rows)
    mixed = pl.pallas_call(
        mix_later_kernel, in_specs=ins + [anywhere], out_specs=outs, name="mix_later", **params
    )(*arrays, after)
    ins, outs = specs(taps)
    return pl.pallas_call(
        mix_first_kernel,
        in_specs=ins + [first] + [anywhere] * 3,
        out_specs=outs,
        input_output_aliases={7: 0, 8: 1, 9: 2},
        name="mix_first",
        **params,
    )(*arrays, earlier, *mixed)


def softened(queries, keys, rows, heats, live):
    f32 = jnp.float32
    queries = [unit(query).astype(jnp.bfloat16) for query in queries]
    scores = [jnp.dot(*pair, preferred_element_type=f32) for pair in zip(queries, keys)]
    weights = [jnp.where(live, jnp.exp2(s * heat), 0.0) for s, heat in zip(scores, heats)]
    totals = [jnp.sum(weight, axis=-1, keepdims=True) for weight in weights]
    sums = [
        jnp.dot(weight.astype(jnp.bfloat16), rows_of, preferred_element_type=f32)
        for weight, rows_of in zip(weights, rows)
    ]
    return [part / total for part, total in zip(sums, totals)]


def together(count, high):
    most = 8 if high <= 128 else 4
    return max(size for size in range(1, most + 1) if count % size == 0)


def masks(offsets, first, slots, tokens, positions):
    place = lax.broadcasted_iota(jnp.int32, (tokens, positions), 1)
    return jnp.concatenate([place < offsets[first + slot] for slot in range(slots)], 0)


def attend_heads(info, temps, keys, rows, places, first, last):
    positions = keys.shape[2]
    slots, tokens = places[0][:2]
    each = slots * tokens
    live = masks(info, info.shape[0] - AHEAD, slots, tokens, positions)
    live = jnp.concatenate([live] * len(places), 0)

    batch = together(last - first, each * len(places))

    def some(step, carry):
        heads = [first + step * batch + at for at in range(batch)]
        queries = []
        for head in heads:
            parts = [load(head).astype(jnp.float32) for _, _, load, _ in places]
            queries.append(jnp.concatenate([part.reshape(each, HEAD_DIM) for part in parts], 0))
        heats = [temps[head] * (LOG2E / HEAD_DIM) for head in heads]
        done = softened(queries, [keys[h] for h in heads], [rows[h] for h in heads], heats, live)
        for head, block in zip(heads, done):
            for place, (_, _, _, store) in enumerate(places):
                part = block[place * each : (place + 1) * each].reshape(slots, tokens, HEAD_DIM)
                store(head, part.astype(jnp.bfloat16))
        return carry

    lax.fori_loop(0, (last - first) // batch, some, 0)


def columns(head):
    return pl.ds(pl.multiple_of(head * HEAD_DIM, HEAD_DIM), HEAD_DIM)


def loader(ref, shift, *at):
    return lambda head: ref[at + (slice(None), slice(None), columns(head - shift))]


def storer(ref, shift, *at):
    def store(head, block):
        ref[at + (slice(None), slice(None), columns(head - shift))] = block

    return store


def near_kernel(info, temps, keys, rows, _, near, out):
    half, slots, tokens, _ = near.shape
    places = [(slots, tokens, loader(near, 0, at), storer(out, 0, at)) for at in range(half)]
    attend_heads(info, temps, keys, rows, places, 0, keys.shape[0])


def first_kernel(tail, info, temps, keys, rows, _, queries, rest, out, kept):
    slots, tokens, _ = queries.shape
    heads = keys.shape[0]
    split = heads - 2 * tail
    places = [(slots, tokens, loader(queries, 0), storer(out, 0))]
    attend_heads(info, temps, keys, rows, places, 0, heads - tail)
    part = slice(split * HEAD_DIM, (split + tail) * HEAD_DIM)
    home = on_hot_half(info, out_peers(heads, tail))

    kept[...] = out[:, :, part]

    @pl.when(jnp.logical_not(home))
    def _():
        out[:, :, part] = rest[...]


def second_kernel(tail, first, count, info, temps, keys, rows, extra, _, *refs):
    queries, later, kept = (refs[at * count : (at + 1) * count] for at in range(3))
    outs, held = refs[3 * count : 4 * count], refs[-1]
    slots, tokens, _ = queries[0].shape
    heads = keys.shape[0]
    split = heads - 2 * tail
    part = slice(tail * HEAD_DIM, 2 * tail * HEAD_DIM)
    home = on_hot_half(info, out_peers(heads, tail))

    @pl.when(home)
    def _():
        for at in range(count):
            held[at] = later[at][:, :, split * HEAD_DIM :]
            outs[at][:, :, part] = extra[first + at]

    @pl.when(jnp.logical_not(home))
    def _():
        for at in range(count):
            held[at] = queries[at][:, :, (split + tail) * HEAD_DIM :]
            outs[at][:, :, part] = kept[at][...]

    places = [
        (slots, tokens, loader(held, heads - tail, at), storer(outs[at], heads - tail))
        for at in range(count)
    ]
    attend_heads(info, temps, keys, rows, places, heads - tail, heads)


def out_peers(heads, tail):
    return 2 * (heads // tail)


def on_hot_half(info, peers):
    half = peers // 2
    return (lax.axis_index("pos") >= half) == (info[info.shape[0] - 1] >= half)


def attend(kernel, name, widths, info, temps, keys, rows, refs, unread, arrays, scratch=()):
    scalars = pl.BlockSpec(memory_space=pltpu.SMEM)
    vector = pl.BlockSpec(memory_space=pltpu.VMEM)
    anywhere = pl.BlockSpec(memory_space=pl.ANY)
    leading = arrays[0].shape[:-1]
    return pl.pallas_call(
        kernel,
        in_specs=[scalars, scalars, vector, vector]
        + [vector] * len(refs)
        + [anywhere]
        + [vector] * len(arrays),
        out_specs=[vector] * len(widths),
        out_shape=[
            jax.ShapeDtypeStruct(leading + (width * HEAD_DIM,), jnp.bfloat16) for width in widths
        ],
        scratch_shapes=list(scratch),
        compiler_params=pltpu.CompilerParams(vmem_limit_bytes=16 * MIB),
        cost_estimate=cost(ATTEND_FLOPS),
        name=name,
    )(info, temps, keys, rows, *refs, unread, *arrays)


def holds(info, done):
    hot = info[info.shape[0] - 1]
    apart = jnp.bitwise_xor(lax.axis_index("pos"), hot)
    for bit in done:
        apart -= apart // (1 << bit) % 2 * (1 << bit)
    return apart == 0


def cut_kernel(stage, ways, info, *refs):
    sources, (sent, kept) = refs[: -2 * len(ways) - 1], (refs[-2 * len(ways) : -len(ways)], refs[-len(ways) :])
    for at, (start, _, order) in enumerate(ways):
        count = sent[at].shape[0]
        mine = lax.axis_index("pos") // (1 << order[stage]) % 2
        if stage:
            have = holds(info, order[: stage - 1])
            choices = [(have, sources[2 * at]), (jnp.logical_not(have), sources[2 * at + 1])]
            start = 0
        else:
            choices = [(True, sources[0])]
        for whether, source in choices:

            @pl.when(whether)
            def _():
                sent[at][...] = source[pl.ds(start + (1 - mine) * count, count)]
                kept[at][...] = source[pl.ds(start + mine * count, count)]


def cut(stage, ways, info, sources, after):
    _, positions, wide = sources[0].shape
    vector = pl.BlockSpec(memory_space=pltpu.VMEM)
    halves_of = [
        jax.ShapeDtypeStruct((count >> (stage + 1), positions, wide), sources[0].dtype)
        for _, count, _ in ways
    ]
    outs = pl.pallas_call(
        functools.partial(cut_kernel, stage, ways),
        in_specs=[pl.BlockSpec(memory_space=pltpu.SMEM)]
        + [vector] * len(sources)
        + [pl.BlockSpec(memory_space=pl.ANY)],
        out_specs=[vector] * (2 * len(ways)),
        out_shape=halves_of * 2,
        compiler_params=pltpu.CompilerParams(vmem_limit_bytes=16 * MIB),
        cost_estimate=cost(1000),
        name="cut",
    )(info, *sources, after)
    return outs[: len(ways)], outs[len(ways) :]


def extra_kernel(ways, info, temps, *refs):
    rows, near, far = refs[: 2 * len(ways)], refs[2 * len(ways) + 1], refs[2 * len(ways) + 2 : -2]
    near_out, far_out = refs[-2:]
    half, extras, tokens, wide = near.shape
    me = lax.axis_index("pos")
    live = masks(info, info.shape[0] - AHEAD + HOT, extras, tokens, rows[0].shape[1])
    live = jnp.concatenate([live] * half, 0)
    values, heats = [], []
    pieces = share_of(me, half, temps.shape[0])
    for at, ((_, _, order), (first, count)) in enumerate(zip(ways, pieces)):
        have = holds(info, order[:-1])
        for head in range(count):
            values.append(jnp.where(have, rows[2 * at][head], rows[2 * at + 1][head]))
            heats.append(temps[first + head] * (LOG2E / HEAD_DIM))
    keyed = [unit(valued.astype(jnp.float32)).astype(jnp.bfloat16).T for valued in values]
    for side in range(2):
        queries = []
        for head in range(len(values)):
            cols = slice(head * HEAD_DIM, (head + 1) * HEAD_DIM)
            query = [source[:, :, cols] for source in far] if side else [near[:, :, :, cols]]
            query = [part.astype(jnp.float32).reshape(-1, HEAD_DIM) for part in query]
            queries.append(jnp.concatenate(query, 0))
        for head, done in enumerate(softened(queries, keyed, values, heats, live)):
            cols = slice(head * HEAD_DIM, (head + 1) * HEAD_DIM)
            done = done.reshape(half, extras, tokens, HEAD_DIM).astype(jnp.bfloat16)
            (far_out if side else near_out)[:, :, :, cols] = done


def attend_extra(ways, info, temps, rows, after, near, far, wide):
    half, extras, tokens, columns = near.shape
    scalars = pl.BlockSpec(memory_space=pltpu.SMEM)
    return pl.pallas_call(
        functools.partial(extra_kernel, ways),
        grid=(1,),
        in_specs=[
            scalars,
            scalars,
        ]
        + [pl.BlockSpec(array.shape, lambda i: (0, 0, 0)) for array in rows]
        + [
            pl.BlockSpec(memory_space=pl.ANY),
            pl.BlockSpec((half, extras, tokens, wide), lambda i: (0, 0, 0, columns // wide - 1)),
        ]
        + [pl.BlockSpec((extras, tokens, wide), lambda i: (0, 0, columns // wide - 2))] * half,
        out_specs=[pl.BlockSpec((half, extras, tokens, wide), lambda i: (0, 0, 0, 0))] * 2,
        out_shape=[jax.ShapeDtypeStruct((half, extras, tokens, wide), jnp.bfloat16)] * 2,
        compiler_params=pltpu.CompilerParams(vmem_limit_bytes=16 * MIB),
        cost_estimate=cost(ATTEND_FLOPS),
        name="attend_extra",
    )(info, temps, *rows, after, near, *far)


def route(info, peers, slots, extras, rows, blocks, sites):
    me = lax.axis_index("pos")
    ahead = info.shape[0] - AHEAD
    hot_at = info.shape[0] - 1

    def clear(at, carry):
        info[at] = -1
        return carry

    lax.fori_loop(0, info.shape[0], clear, 0)
    for window in range(blocks.shape[0]):
        block = blocks[window]
        count = jnp.int32(0)
        for slot in range(HOT - 1):
            count += (info[block * HOT + slot] >= 0).astype(jnp.int32)
        info[block * HOT + count] = window

        @pl.when(count == HOT - 1)
        def _():
            info[hot_at] = block

    hot = info[hot_at]

    def offset(entry):
        window = info[entry]
        site = sites[jnp.maximum(window, 0)]
        return jnp.where(window >= 0, site - rows * (entry // HOT), rows)

    for slot in range(HOT):
        info[ahead + slot] = offset(me * HOT + slot)
    for extra in range(extras):
        info[ahead + HOT + extra] = offset(hot * HOT + slots + extra)


def paths(half, heads):
    order = tuple(range(half.bit_length() - 1))
    if heads // half % 2:
        return [(0, heads, order)]
    return [(0, heads // 2, order), (heads // 2, heads // 2, order[::-1])]


def share_of(index, half, heads):
    pieces = []
    for start, count, order in paths(half, heads):
        for bit in order:
            count //= 2
            start += index // (1 << bit) % 2 * count
        pieces.append((start, count))
    return pieces


def columns_of(piece):
    start, count = piece
    wide = count * HEAD_DIM
    if isinstance(start, int):
        return pl.ds(start * HEAD_DIM, wide)
    return pl.ds(pl.multiple_of(start * HEAD_DIM, wide), wide)


def copied(copies, sems):
    copies = [pltpu.make_async_copy(*pair, sems.at[at]) for at, pair in enumerate(copies)]
    for copy in copies:
        copy.start()
    for copy in copies:
        copy.wait()


def message(info, queries, peer, out, wide, extras, start, count, with_extras):
    slots, _, held = out.shape
    hot = info[info.shape[0] - 1]
    copies = []
    for slot in range(slots):
        window = jnp.maximum(info[peer * HOT + slot], 0)
        source = queries.at[window, :, pl.ds(start, count)]
        copies.append((source, out.at[slot, :, pl.ds(0, count)]))
    half = queries.shape[2] // wide
    for extra in range(extras if held > count else 0):
        at = 0
        for first, size in share_of(peer, half, queries.shape[2] // HEAD_DIM):
            window = info[hot * HOT + slots + extra]
            if with_extras is not None:
                window = jnp.where(with_extras, window, jnp.maximum(info[peer * HOT + extra], 0))
                first = jnp.where(with_extras, first, (start + count) // HEAD_DIM + at)
            source = queries.at[window, :, columns_of((first, size))]
            target = out.at[extra, :, pl.ds(count + at * HEAD_DIM, size * HEAD_DIM)]
            copies.append((source, target))
            at += size
    return copies


def far_steps(half):
    order = [at for pair in zip(range(half // 2, half), range(half // 2)) for at in pair]
    return [half + at for at in order]


def far_copies(info, queries, steps, far, rest, wide, extras):
    half = queries.shape[2] // wide
    me = lax.axis_index("pos")
    away = jnp.logical_not(on_hot_half(info, 2 * half))
    chans = queries.shape[2]
    copies = []
    for step, out, other in zip(steps, far, rest):
        peer = jnp.bitwise_xor(me, step)
        copies += message(info, queries, peer, out, wide, extras, 0, chans - wide, away)
        copies += message(info, queries, peer, other, wide, extras, chans - wide, wide, None)
    return copies


def pack_kernel(extras, rows, wide, blocks, sites, queries, _, info, near, *refs):
    half, slots, _, _ = near.shape
    outs, (sems, blocks_held, sites_held, pair) = refs[:-4], refs[-4:]
    count = len(outs) // 2
    copied([(blocks, blocks_held), (sites, sites_held)], pair)
    route(info, 2 * half, slots, extras, rows, blocks_held, sites_held)
    base = jnp.bitwise_and(lax.axis_index("pos"), half)
    chans = queries.shape[2]
    steps = far_steps(half)
    copies = far_copies(info, queries, steps, outs[:count], outs[count:], wide, extras)
    for at in range(half):
        copies += message(info, queries, base + at, near.at[at], wide, extras, 0, chans, None)
    copied(copies, sems)


def far_shapes(queries, slots, wide, count):
    _, tokens, chans = queries.shape
    return [jax.ShapeDtypeStruct((slots, tokens, chans), queries.dtype)] * count + [
        jax.ShapeDtypeStruct((slots, tokens, wide), queries.dtype)
    ] * count


def pack(blocks, sites, queries, tail, rows, half, slots, extras, wide, count):
    windows, tokens, chans = queries.shape
    scalars = pl.BlockSpec(memory_space=pltpu.SMEM)
    vector = pl.BlockSpec(memory_space=pltpu.VMEM)
    anywhere = pl.BlockSpec(memory_space=pl.ANY)
    info, near, *far = pl.pallas_call(
        functools.partial(pack_kernel, extras, rows, wide),
        in_specs=[anywhere] * 4,
        out_specs=[scalars] + [vector] * (1 + 2 * count),
        out_shape=[
            jax.ShapeDtypeStruct((2 * half * HOT + AHEAD,), jnp.int32),
            jax.ShapeDtypeStruct((half, slots, tokens, chans + wide), queries.dtype),
        ]
        + far_shapes(queries, slots, wide, count),
        scratch_shapes=[
            pltpu.SemaphoreType.DMA(((half + count) * (slots + 2 * extras) + count * slots,)),
            pltpu.SMEM((windows,), jnp.int32),
            pltpu.SMEM((windows,), jnp.int32),
            pltpu.SemaphoreType.DMA((2,)),
        ],
        compiler_params=pltpu.CompilerParams(vmem_limit_bytes=PACK_VMEM * MIB),
        cost_estimate=cost(PACK_FLOPS),
        name="pack",
    )(blocks, sites, queries, tail)
    return info, near, far[:count], far[count:]


def placed(info, out, sems, pieces):
    def each(act):
        at = 0
        for peer, result, start, count, column, whether in pieces:
            for slot in range(result.shape[0]):
                window = info[peer * HOT + slot]
                source = result.at[slot, :, pl.ds(start, count)]
                target = out.at[jnp.maximum(window, 0), :, pl.ds(column, count)]
                copy = pltpu.make_async_copy(source, target, sems.at[at])
                pl.when(jnp.logical_and(window >= 0, whether))(functools.partial(act, copy))
                at += 1

    each(lambda copy: copy.start())
    return lambda: each(lambda copy: copy.wait())


def unpack_early_kernel(wide, info, near, *refs):
    half = near.shape[0]
    results, (_, out, near_sems, sems) = refs[:half], refs[half:]
    me = lax.axis_index("pos")
    base = jnp.bitwise_and(me, half)
    home = on_hot_half(info, 2 * half)
    chans = out.shape[2]
    split = chans - 2 * wide
    pieces = [(base + at, near.at[at], 0, chans, 0, True) for at in range(half)]
    near_wait = placed(info, out, near_sems, pieces)
    pieces = []
    for at, result in enumerate(results):
        peer = jnp.bitwise_xor(me, far_steps(half)[at])
        pieces.append((peer, result, 0, split, 0, True))
        pieces.append((peer, result, split, wide, split, jnp.logical_not(home)))
    placed(info, out, sems, pieces)()
    near_wait()


def unpack_early(info, near, results, after, shape, wide):
    anywhere = pl.BlockSpec(memory_space=pl.ANY)
    half, slots, _, _ = near.shape
    return pl.pallas_call(
        functools.partial(unpack_early_kernel, wide),
        in_specs=[pl.BlockSpec(memory_space=pltpu.SMEM)]
        + [pl.BlockSpec(memory_space=pltpu.VMEM)] * (1 + half)
        + [anywhere],
        out_specs=anywhere,
        out_shape=jax.ShapeDtypeStruct(shape, near.dtype),
        scratch_shapes=[
            pltpu.SemaphoreType.DMA((half * slots,)),
            pltpu.SemaphoreType.DMA((2 * half * slots,)),
        ],
        compiler_params=pltpu.CompilerParams(vmem_limit_bytes=16 * MIB),
        cost_estimate=cost(1000),
        name="unpack_early",
    )(info, near, *results, after)


def unpack_kernel(wide, steps, info, *refs):
    results, out, semaphores = refs[: len(steps)], refs[len(steps) + 1], refs[len(steps) + 2 :]
    half = out.shape[2] // wide
    split = out.shape[2] - 2 * wide
    home = on_hot_half(info, 2 * half)
    waits = []
    for step, result, sems, extra_sems in zip(steps, results, semaphores[::2], semaphores[1::2]):
        extras = extra_sems.shape[0] // 2
        peer = jnp.bitwise_xor(lax.axis_index("pos"), step)
        pieces = [
            (peer, result, 0, wide, split + wide, True),
            (peer, result, wide, wide, split, home),
        ]
        waits.append(placed(info, out, sems, pieces))
        share = share_of(peer, half, out.shape[2] // HEAD_DIM)
        sources = [result.at[extra, :, pl.ds(wide, wide)] for extra in range(extras)]
        away = jnp.logical_not(home)
        waits.append(placed_extra(info, out, extra_sems, sources, share, away))
    for wait in waits:
        wait()


def placed_extra(info, out, sems, sources, share, whether):
    extras = len(sources)
    hot = info[info.shape[0] - 1]

    def each(act):
        for extra, source in enumerate(sources):
            window = info[hot * HOT + HOT - extras + extra]
            at = 0
            for place, piece in enumerate(share):
                part = source.at[:, pl.ds(at * HEAD_DIM, piece[1] * HEAD_DIM)]
                target = out.at[window, :, columns_of(piece)]
                copy = pltpu.make_async_copy(part, target, sems.at[2 * extra + place])
                pl.when(whether)(functools.partial(act, copy))
                at += piece[1]

    each(lambda copy: copy.start())
    return lambda: each(lambda copy: copy.wait())


def unpack_extra_kernel(info, near, _, out, *sems):
    half, extras, _, _ = near.shape
    home = on_hot_half(info, 2 * half)
    waits = []
    for at in range(half):
        sources = [near.at[at, extra] for extra in range(extras)]
        share = share_of(at, half, out.shape[2] // HEAD_DIM)
        waits.append(placed_extra(info, out, sems[at], sources, share, home))
    for wait in waits:
        wait()


def unpack(kernel, name, info, results, so_far, semaphores):
    anywhere = pl.BlockSpec(memory_space=pl.ANY)
    vector = pl.BlockSpec(memory_space=pltpu.VMEM)
    return pl.pallas_call(
        kernel,
        in_specs=[pl.BlockSpec(memory_space=pltpu.SMEM)] + [vector] * len(results) + [anywhere],
        out_specs=anywhere,
        out_shape=jax.ShapeDtypeStruct(so_far.shape, so_far.dtype),
        input_output_aliases={1 + len(results): 0},
        scratch_shapes=[pltpu.SemaphoreType.DMA((count,)) for count in semaphores],
        compiler_params=pltpu.CompilerParams(vmem_limit_bytes=16 * MIB),
        cost_estimate=cost(UNPACK_FLOPS),
        name=name,
    )(info, *results, so_far)


def exchanged(value, step):
    peers = lax.axis_size("pos")
    if step == 0:
        return value
    return lax.ppermute(value, "pos", [(i, i ^ step) for i in range(peers)])


def exchanged_near(value):
    peers = lax.axis_size("pos")
    half = peers // 2
    groups = [list(range(half)), list(range(half, peers))]
    return lax.all_to_all(value, "pos", 0, 0, axis_index_groups=groups, tiled=True)


def shards(gate_stream, key_stream, value_stream, filters, temps, queries, blocks, sites):
    rows, chans = gate_stream.shape
    taps = filters.shape[1]
    peers = lax.axis_size("pos")
    me = lax.axis_index("pos").astype(jnp.int32)
    windows = blocks.shape[0]
    heads = chans // HEAD_DIM
    extras = 2
    slots = HOT - extras
    half = peers // 2

    last = slice(rows - taps, rows)
    tail = key_stream[last].astype(jnp.float32) * value_stream[last].astype(jnp.float32)
    tail = tail.astype(jnp.bfloat16)
    earlier = lax.ppermute(tail, "pos", [(i, i + 1) for i in range(peers - 1)])
    wide = chans // half
    share = heads // half
    info, near, far, rest = pack(
        blocks, sites, queries, tail, rows, half, slots, extras, wide, half
    )
    far = [exchanged(sent, step) for step, sent in zip(far_steps(half), far)]
    near = exchanged_near(near)
    hyena_out, valued, keyed = mix(
        gate_stream, key_stream, value_stream, earlier, filters, info
    )
    own = (info, temps, keyed, valued)

    ways = paths(half, heads)

    def halved(stage, sources, after):
        moved, kept_rows = cut(stage, ways, info, sources, after)
        pairs = []
        for (_, _, order), out, stays in zip(ways, moved, kept_rows):
            pairs += [stays, exchanged(out, 1 << order[stage])]
        return pairs, moved[0]

    def first(at, after):
        kernel = functools.partial(first_kernel, share)
        arrays = [far[at], rest[at]]
        result, back = attend(
            kernel, "attend_first", [heads - share, share], *own, [], after, arrays
        )
        sent.append(exchanged(result, far_steps(half)[at]))
        kept.append(back)
        return result

    def second(at, count, after):
        kernel = functools.partial(second_kernel, share, at, count)
        some = slice(at, at + count)
        arrays = far[some] + sent[some] + kept[some]
        scratch = [pltpu.VMEM((count,) + kept[at].shape, jnp.bfloat16)]
        results = attend(
            kernel, "attend_second", [2 * share] * count, *own, [extra], after, arrays, scratch
        )
        late.extend(
            exchanged(result, far_steps(half)[at + more]) for more, result in enumerate(results)
        )
        return results[0]

    sent, kept, late = [], [], []
    hot_rows, after = halved(0, [valued], valued)
    after = first(0, after)
    (near_results,) = attend(near_kernel, "attend_near", [heads], *own, [], after, [near])
    near_out, after = exchanged_near(near_results), near_results
    for stage in range(1, half.bit_length() - 1):
        hot_rows, after = halved(stage, hot_rows, after)
    for at in range(1, half):
        after = first(at, after)
    near_extra, extra = attend_extra(ways, info, temps, hot_rows, after, near, far, wide)
    near_extra, after = exchanged_near(near_extra), extra
    for at in range(half):
        after = second(at, 1, after)
    so_far = unpack_early(info, near_out, sent, after, queries.shape, wide)
    count = [2 * extras] * half
    so_far = unpack(unpack_extra_kernel, "unpack_extra", info, [near_extra], so_far, count)
    for at in range(0, half, 2):
        kernel = functools.partial(unpack_kernel, wide, far_steps(half)[at : at + 2])
        results = late[at : at + 2]
        so_far = unpack(kernel, "unpack", info, results, so_far, [2 * slots, 2 * extras] * 2)
    return (hyena_out, so_far)


def solution(mesh):
    placed = (
        P(("groups", "pos"), "mp"),
        P(("groups", "pos"), "mp"),
        P(("groups", "pos"), "mp"),
        P("mp", None),
        P("mp"),
        P("groups", "pos", "mp"),
        P("groups"),
        P("groups"),
    )
    return jax.shard_map(
        shards,
        mesh=mesh,
        in_specs=placed,
        out_specs=(P(("groups", "pos"), "mp"), P("groups", "pos", "mp")),
        check_vma=False,
    )
```
